32 devices in a mesh: wide: 16 (over z, y, x), narrow: 2 (over core).
Axes of the slice: x: 2, y: 2, z: 4, core: 2. Of those that a mesh axis runs over, the one named last changes fastest.
Arguments:
- rhs: float32 [384, 64, 128], P(('wide', 'narrow')), may hold values from -8 to 8
- pivot_inv: float32 [384, 128, 128], P(('wide', 'narrow')), may hold values from -0.5 to 0.5
- lower_gain: float32 [384, 128, 128], P(('wide', 'narrow')), may hold values from -1 to 1
- upper_gain: float32 [384, 128, 128], P(('wide', 'narrow')), may hold values from -1 to 1
Outputs:
- solution: float32 [384, 64, 128], P(('wide', 'narrow'))
The draws below stay inside these ranges and needn't reach their ends.
All inputs are finite; a program needn't handle non-finite values.
Results may differ from the reference program's by a relative error of at most 0.0003.
Values sent between devices are 32-bit elements; how exact they have to be, the bound alone decides.
A program may use at most 128 MiB of HBM per device.

```python
import math
import jax
import jax.numpy as jnp
from jax import lax

B = 128
R = 64
PANEL_COUNT_FULL = 384


def rotation_frames(key, count):
    levels = B.bit_length() - 1
    angles = jax.random.uniform(key, (2 * levels, count, B // 2), minval=-math.pi, maxval=math.pi)
    basis = jnp.broadcast_to(jnp.eye(B, dtype=jnp.float32), (count, B, B))
    for segment in range(2 * levels):
        stride = 2 ** (segment % levels)
        shaped = basis.reshape(count, B, B // (2 * stride), 2, stride)
        turn = angles[segment].reshape(count, 1, B // (2 * stride), stride)
        cosine = jnp.cos(turn)
        sine = jnp.sin(turn)
        first = shaped[:, :, :, 0, :]
        second = shaped[:, :, :, 1, :]
        basis = jnp.stack((cosine * first - sine * second, sine * first + cosine * second), axis=3).reshape(count, B, B)
    return basis


def gain_stack(key, slow_eighths, spread, ascending):
    sampler_seeds = jax.random.split(key, 7)
    gradual_portion = (jax.random.randint(sampler_seeds[0], (B,), 0, 8) < slow_eighths).astype(jnp.float32)
    slow_rate = 1.0 / (PANEL_COUNT_FULL * jnp.exp(jax.random.uniform(sampler_seeds[1], (B,), minval=0.0, maxval=math.log(6.0))))
    fast_rate = jnp.exp(jax.random.uniform(sampler_seeds[2], (B,), minval=math.log(0.02), maxval=math.log(0.2)))
    attenuation_speed = gradual_portion * slow_rate + (1.0 - gradual_portion) * fast_rate
    perturbation_magnitude = jax.random.uniform(sampler_seeds[3], (PANEL_COUNT_FULL, B), minval=1.0 - spread, maxval=1.0 + spread)
    spike_multiplier = jnp.where(jax.random.uniform(sampler_seeds[4], (PANEL_COUNT_FULL, 1)) < 3.0 / PANEL_COUNT_FULL, 0.7, 1.0)
    shrinkage_multiplier = jnp.exp(-attenuation_speed * perturbation_magnitude) * (gradual_portion * spike_multiplier + 1.0 - gradual_portion)
    frames = rotation_frames(sampler_seeds[5], PANEL_COUNT_FULL + 1)
    if ascending:
        left_frame = frames[:-1]
        right_frame = frames[1:]
    else:
        left_frame = frames[1:]
        right_frame = frames[:-1]
    core = jnp.einsum('kij,klj->kil', left_frame * shrinkage_multiplier[:, None, :], right_frame, precision=lax.Precision.HIGHEST)
    jitter = jax.random.normal(sampler_seeds[6], (PANEL_COUNT_FULL, B, B)) * (0.5 / math.sqrt(PANEL_COUNT_FULL * B))
    return jnp.clip(core + jitter, -1.0, 1.0).astype(jnp.float32)


def draw_lower_gain(key, part):
    key = jax.random.fold_in(key, 3)
    return gain_stack(key, 4, 0.5, True)


def draw_upper_gain(key, part):
    key = jax.random.fold_in(key, 5)
    return gain_stack(key, 4, 0.5, False)


def block_scale(key, extent, cuts, least, largest):
    def one(position, shards_of):
        heights = jax.random.uniform(jax.random.fold_in(jax.random.fold_in(key, 6), position), (shards_of,), jnp.float32, least / len(cuts), largest / len(cuts))
        return jnp.repeat(jnp.exp(heights), extent[position] // shards_of).reshape((-1,) + (1,) * (len(extent) - position - 1))

    level = one(*cuts[0])
    for cut in cuts[1:]:
        level = level * one(*cut)
    return level


def centred(rng, shape, deviation, reach, cuts=(), kind=jnp.bfloat16):
    values = deviation * jax.random.normal(rng, shape, jnp.float32)
    if cuts:
        values = values * block_scale(rng, shape, cuts, -0.22, 0.18)
    return jnp.clip(values, -reach, reach).astype(kind)


def setup_inputs(seed: int = 0) -> dict:
    key_list = jax.random.split(jax.random.key(seed), 5)
    return {
        "rhs": centred(key_list[0], (PANEL_COUNT_FULL, R, B), 1.0, 8.0, ((0, 32),), jnp.float32),
        "pivot_inv": centred(key_list[1], (PANEL_COUNT_FULL, B, B), B ** -0.5, 0.5, ((0, 32),), jnp.float32),
        "lower_gain": draw_lower_gain(jax.random.fold_in(key_list[4], 71), 0),
        "upper_gain": draw_upper_gain(jax.random.fold_in(key_list[4], 71), 0),
    }


def reference(rhs, pivot_inv, lower_gain, upper_gain):
    highest = lax.Precision.HIGHEST
    scaled = jnp.einsum("krb,kbc->krc", rhs, pivot_inv, precision=highest)

    def stepper(carry, item):
        gain, offset = item
        fresh = offset - jnp.dot(carry, gain, precision=highest)
        return fresh, fresh

    start = jnp.zeros((rhs.shape[1], rhs.shape[2]), jnp.float32)
    _, forward = lax.scan(stepper, start, (lower_gain, scaled))
    _, solution = lax.scan(stepper, start, (upper_gain, forward), reverse=True)
    return solution
```

```python
import functools

import jax
import jax.numpy as jnp
from jax import lax
from jax.experimental import pallas as pl
from jax.experimental.pallas import tpu as pltpu
from jax.sharding import PartitionSpec as P

MESH = pl.DeviceIdType.MESH


def halves(value):
    high = value.astype(jnp.bfloat16)
    low = (value - high.astype(jnp.float32)).astype(jnp.bfloat16)
    return high, low


def right_side(value):
    high, low = halves(value)
    row = jnp.concatenate([high, low], axis=1)
    return jnp.concatenate([row, row], axis=0)


def left_side(value):
    high, low = halves(value)
    return jnp.concatenate([high, low], axis=1)


def fold(value, width):
    return value[:, :width] + value[:, width:]


def product(left, right):
    wide = jnp.dot(left_side(left), right_side(right), preferred_element_type=jnp.float32)
    return fold(wide, right.shape[1])


def kernel(
    levels, rhs, pivot, lower, upper, out, ahead, tails, maps, group, fp, fq, fs, send_sem, recv_sem
):
    rows, sides, size = rhs.shape
    m0, c0, w0, b0, n0, end = 0, size, size + sides, 2 * size + sides, 2 * (size + sides), 3 * size + 2 * sides
    names = ("wide", "narrow")
    place = {name: lax.axis_index(name) for name in names}

    def partner(level):
        axis, stride = levels[level]
        mine = place[axis]
        side = lax.rem(lax.div(mine, stride), 2)
        other = mine + stride - 2 * stride * side
        return side, tuple(other if name == axis else place[name] for name in names)

    barrier = pltpu.get_barrier_semaphore()
    for level in range(len(levels)):
        pl.semaphore_signal(barrier, inc=1, device_id=partner(level)[1], device_id_type=MESH)

    scaled = [product(rhs[i], pivot[i]) for i in range(rows)]
    front = jnp.concatenate([-lower[0], scaled[0]], axis=0)
    ahead[0] = front
    back = -upper[rows - 1]
    tails[rows - 1, size + sides :] = back
    for i in range(1, rows):
        step = product(front, lower[i])
        front = jnp.concatenate([-step[:size], scaled[i] - step[size:]], axis=0)
        ahead[i] = front
        back = -product(back, upper[rows - 1 - i])
        tails[rows - 1 - i, size + sides :] = back
    total = front
    tails[rows - 1, : size + sides] = total
    for i in range(rows - 2, -1, -1):
        total = ahead[i] - product(total, upper[i])
        tails[i, : size + sides] = total

    pl.semaphore_wait(barrier, len(levels))

    def exchange(level):
        side, other = partner(level)
        span = pl.ds(c0, n0 - c0) if level == len(levels) - 1 else pl.ds(0, end)
        return pltpu.make_async_remote_copy(
            src_ref=group.at[level, side, span],
            dst_ref=group.at[level, side, span],
            send_sem=send_sem.at[level],
            recv_sem=recv_sem.at[level],
            device_id=other,
            device_id_type=MESH,
        )

    side = partner(0)[0]
    group[0, side, :c0] = ahead[rows - 1, :size]
    group[0, side, c0:w0] = ahead[rows - 1, size:]
    group[0, side, w0:n0] = tails[0, : size + sides]
    group[0, side, n0:] = tails[0, size + sides :]
    copy = exchange(0)
    copy.start()

    for i in range(rows):
        w_high, w_low = halves(tails[i, :size])
        n_high, n_low = halves(tails[i, size + sides :])
        maps[i] = jnp.concatenate(
            [jnp.concatenate([w_high, w_low], axis=1), jnp.concatenate([n_high, n_low], axis=1)], axis=0
        )
    eye = (
        lax.broadcasted_iota(jnp.int32, (size, size), 0) == lax.broadcasted_iota(jnp.int32, (size, size), 1)
    ).astype(jnp.float32)
    fp[:size] = eye
    fp[size:] = jnp.zeros((sides, size), jnp.float32)
    fq[...] = eye
    fs[...] = jnp.zeros((size + sides, size), jnp.float32)

    for level in range(len(levels) - 1):
        copy.wait()
        side = partner(level)[0]
        first, second = group.at[level, 0], group.at[level, 1]
        front = first[m0:w0]
        joined = jnp.dot(
            left_side(front),
            jnp.concatenate([right_side(second[m0:c0]), right_side(second[w0:b0])], axis=1),
            preferred_element_type=jnp.float32,
        )
        onward = fold(joined[:, : 2 * size], size)
        turned = fold(joined[:, 2 * size :], size)
        turned = jnp.concatenate([turned[:size], turned[size:] + second[b0:n0]], axis=0)
        returned = product(jnp.concatenate([turned, second[n0:]], axis=0), first[n0:])
        following = partner(level + 1)[0]
        group[level + 1, following, m0:c0] = onward[:size]
        group[level + 1, following, c0:w0] = onward[size:] + second[c0:w0]
        group[level + 1, following, w0:n0] = first[w0:n0] + returned[: size + sides]
        group[level + 1, following, n0:] = returned[size + sides :]
        copy = exchange(level + 1)
        copy.start()

        @pl.when(side == 0)
        def _():
            more = product(jnp.concatenate([turned, second[n0:]], axis=0), fq[...])
            fs[...] = fs[...] + more[: size + sides]
            fq[...] = more[size + sides :]

        @pl.when(side == 1)
        def _():
            more = product(front, fp[:size])
            fp[size:] = fp[size:] + more[size:]
            fp[:size] = more[:size]
            more = product(front, fs[:size])
            fs[size:] = fs[size:] + more[size:]
            fs[:size] = more[:size]

    copy.wait()
    level = len(levels) - 1
    side = partner(level)[0]
    enter = group[level, 0, c0:w0]
    leave = product(enter, group[level, 1, w0:b0]) + group[level, 1, b0:n0]
    enter = jnp.where(side == 1, enter, 0.0)
    leave = jnp.where(side == 0, leave, 0.0)
    x_in = product(enter, fp[:size]) + fp[size:]
    y_in = product(leave, fq[...]) + product(enter, fs[:size]) + fs[size:]
    x_high, x_low = halves(x_in)
    y_high, y_low = halves(y_in)
    left = jnp.concatenate(
        [jnp.concatenate([x_high, y_high], axis=1), jnp.concatenate([x_low, y_low], axis=1)], axis=0
    )
    for i in range(rows):
        both = fold(jnp.dot(left, maps[i], preferred_element_type=jnp.float32), size)
        out[i] = tails[i, size : size + sides] + both[:sides] + both[sides:]


def on_device(levels, rhs, pivot_inv, lower_gain, upper_gain):
    rows, sides, size = rhs.shape
    depth = len(levels)
    span = 3 * size + 2 * sides
    whole = pl.BlockSpec(memory_space=pltpu.VMEM)
    return pl.pallas_call(
        functools.partial(kernel, levels),
        out_shape=jax.ShapeDtypeStruct(rhs.shape, jnp.float32),
        in_specs=[whole] * 4,
        out_specs=whole,
        scratch_shapes=[
            pltpu.VMEM((rows, size + sides, size), jnp.float32),
            pltpu.VMEM((rows, 2 * size + sides, size), jnp.float32),
            pltpu.VMEM((rows, 2 * size, 2 * size), jnp.bfloat16),
            pltpu.VMEM((depth, 2, span, size), jnp.float32),
            pltpu.VMEM((size + sides, size), jnp.float32),
            pltpu.VMEM((size, size), jnp.float32),
            pltpu.VMEM((size + sides, size), jnp.float32),
            pltpu.SemaphoreType.DMA((depth,)),
            pltpu.SemaphoreType.DMA((depth,)),
        ],
        compiler_params=pltpu.CompilerParams(
            collective_id=0, has_side_effects=True, vmem_limit_bytes=40 * 2**20
        ),
    )(rhs, pivot_inv, lower_gain, upper_gain)


def solution(mesh):
    levels = []
    for axis in ("narrow", "wide"):
        stride = 1
        while stride < mesh.shape[axis]:
            levels.append((axis, stride))
            stride *= 2
    placed = P(("wide", "narrow"), None, None)
    return jax.shard_map(
        functools.partial(on_device, tuple(levels)),
        mesh=mesh,
        in_specs=(placed,) * 4,
        out_specs=placed,
        check_vma=False,
    )
```

```python
import functools

import jax
import jax.numpy as jnp
from jax import lax
from jax.experimental import pallas as pl
from jax.experimental.pallas import tpu as pltpu
from jax.sharding import PartitionSpec as P

MESH = pl.DeviceIdType.MESH
PIECE = 3
PARTS = 2


def halves(value):
    high = value.astype(jnp.bfloat16)
    low = (value - high.astype(jnp.float32)).astype(jnp.bfloat16)
    return high, low


def right_side(value):
    high, low = halves(value)
    row = jnp.concatenate([high, low], axis=1)
    return jnp.concatenate([row, row], axis=0)


def left_side(value):
    high, low = halves(value)
    return jnp.concatenate([high, low], axis=1)


def fold(value, width):
    return value[:, :width] + value[:, width:]


def product(left, right):
    wide = jnp.dot(left_side(left), right_side(right), preferred_element_type=jnp.float32)
    return fold(wide, right.shape[1])


def kernel(
    levels,
    planes,
    rhs_hbm,
    pivot_hbm,
    lower_hbm,
    upper_hbm,
    out,
    rhs,
    pivot,
    lower,
    upper,
    ahead,
    tails,
    maps,
    group,
    fp,
    fq,
    fs,
    enter,
    leave,
    met,
    enter_on,
    leave_on,
    met_on,
    load_sem,
    send_sem,
    recv_sem,
    pass_send_sem,
    pass_recv_sem,
    chain_send_sem,
    chain_recv_sem,
):
    rows, sides, size = rhs.shape
    m0, c0, w0, b0, n0, end = 0, size, size + sides, 2 * size + sides, 2 * (size + sides), 3 * size + 2 * sides
    names = ("wide", "narrow")
    place = {name: lax.axis_index(name) for name in names}
    depth = len(levels)

    loads = {}
    pieces = rows // PIECE
    for step in range(pieces):
        for kind, (source, target) in enumerate(
            ((rhs_hbm, rhs), (pivot_hbm, pivot), (lower_hbm, lower), (upper_hbm, upper))
        ):
            piece = pieces - 1 - step if kind == 3 else step
            span = pl.ds(piece * PIECE, PIECE)
            load = pltpu.make_async_copy(source.at[span], target.at[span], load_sem.at[kind, piece])
            load.start()
            loads[kind, step] = load

    def partner(level):
        axis, stride = levels[level]
        mine = place[axis]
        side = lax.rem(lax.div(mine, stride), 2)
        other = mine + stride - 2 * stride * side
        return side, tuple(other if name == axis else place[name] for name in names)

    hop = lax.axis_size("wide") // planes
    plane = lax.div(place["wide"], hop)
    before = (place["wide"] - hop, place["narrow"])
    after = (place["wide"] + hop, place["narrow"])
    sibling = (place["wide"], 1 - place["narrow"])

    barrier = pltpu.get_barrier_semaphore()
    for level in range(depth):
        pl.semaphore_signal(barrier, inc=1, device_id=partner(level)[1], device_id_type=MESH)

    @pl.when(plane > 0)
    def _():
        pl.semaphore_signal(barrier, inc=1, device_id=before, device_id_type=MESH)

    @pl.when(plane < planes - 1)
    def _():
        pl.semaphore_signal(barrier, inc=1, device_id=after, device_id_type=MESH)

    for i in range(rows):
        if i % PIECE == 0:
            for kind in range(4):
                loads[kind, i // PIECE].wait()
        scaled = product(rhs[i], pivot[i])
        if i == 0:
            front = jnp.concatenate([-lower[0], scaled], axis=0)
            back = -upper[rows - 1]
        else:
            step = product(front, lower[i])
            front = jnp.concatenate([-step[:size], scaled - step[size:]], axis=0)
            back = -product(back, upper[rows - 1 - i])
        ahead[i] = front
        tails[rows - 1 - i, size + sides :] = back
    total = front
    tails[rows - 1, : size + sides] = total
    for i in range(rows - 2, -1, -1):
        total = ahead[i] - product(total, upper[i])
        tails[i, : size + sides] = total

    inner = (plane > 0).astype(jnp.int32) + (plane < planes - 1).astype(jnp.int32)
    pl.semaphore_wait(barrier, depth + inner)

    part = end // (2 * PARTS)

    def exchange(level):
        side, other = partner(level)
        if levels[level][0] == "narrow":
            spans = [pl.ds(0, end)]
        else:
            begin = place["narrow"] * (end // 2)
            spans = [pl.ds(pl.multiple_of(begin + k * part, part), part) for k in range(PARTS)]
        return [
            pltpu.make_async_remote_copy(
                src_ref=group.at[level, side, span],
                dst_ref=group.at[level, side, span],
                send_sem=send_sem.at[level, k],
                recv_sem=recv_sem.at[level, k],
                device_id=other,
                device_id_type=MESH,
            )
            for k, span in enumerate(spans)
        ]

    def finish(level, copies):
        if levels[level][0] == "narrow":
            copies[0].wait()
            return
        side = partner(level)[0]
        begin = place["narrow"] * (end // 2)
        relays = []
        for k, copy in enumerate(copies):
            copy.wait_recv()
            span = pl.ds(pl.multiple_of(begin + k * part, part), part)
            relay = pltpu.make_async_remote_copy(
                src_ref=group.at[level, 1 - side, span],
                dst_ref=group.at[level, 1 - side, span],
                send_sem=pass_send_sem.at[level, k],
                recv_sem=pass_recv_sem.at[level, k],
                device_id=sibling,
                device_id_type=MESH,
            )
            relay.start()
            relays.append(relay)
        for copy in copies:
            copy.wait_send()
        for relay in relays:
            relay.wait()

    side = partner(0)[0]
    group[0, side, :c0] = ahead[rows - 1, :size]
    group[0, side, c0:w0] = ahead[rows - 1, size:]
    group[0, side, w0:n0] = tails[0, : size + sides]
    group[0, side, n0:] = tails[0, size + sides :]
    copies = exchange(0)
    for copy in copies:
        copy.start()

    eye = (
        lax.broadcasted_iota(jnp.int32, (size, size), 0) == lax.broadcasted_iota(jnp.int32, (size, size), 1)
    ).astype(jnp.float32)
    fp[:size] = eye
    fp[size:] = jnp.zeros((sides, size), jnp.float32)
    fq[...] = eye
    fs[...] = jnp.zeros((size + sides, size), jnp.float32)

    def hand(kind, source, target, device):
        return pltpu.make_async_remote_copy(
            src_ref=source,
            dst_ref=target,
            send_sem=chain_send_sem.at[kind],
            recv_sem=chain_recv_sem.at[kind],
            device_id=device,
            device_id_type=MESH,
        )

    enter_right = hand(0, enter_on, enter, after)
    met_left = hand(1, met_on, met, before)
    leave_left = hand(2, leave_on, leave, before)

    for level in range(depth):
        finish(level, copies)
        side = partner(level)[0]
        first, second = group.at[level, 0], group.at[level, 1]
        front = first[m0:w0]
        joined = jnp.dot(
            left_side(front),
            jnp.concatenate([right_side(second[m0:c0]), right_side(second[w0:b0])], axis=1),
            preferred_element_type=jnp.float32,
        )
        onward = fold(joined[:, : 2 * size], size)
        turned = fold(joined[:, 2 * size :], size)
        turned = jnp.concatenate([turned[:size], turned[size:] + second[b0:n0]], axis=0)
        returned = product(jnp.concatenate([turned, second[n0:]], axis=0), first[n0:])
        following = partner(level + 1)[0] if level < depth - 1 else 0
        group[level + 1, following, m0:c0] = onward[:size]
        group[level + 1, following, c0:w0] = onward[size:] + second[c0:w0]
        group[level + 1, following, w0:n0] = first[w0:n0] + returned[: size + sides]
        group[level + 1, following, n0:] = returned[size + sides :]
        if level < depth - 1:
            copies = exchange(level + 1)
            for copy in copies:
                copy.start()
        else:

            @pl.when(plane == 0)
            def _():
                enter_on[...] = group[depth, 0, c0:w0]
                enter_right.start()

            @pl.when(plane == planes - 1)
            def _():
                met_on[...] = group[depth, 0, w0:n0]
                met_left.start()

        if level == 0:
            for i in range(rows):
                w_high, w_low = halves(tails[i, :size])
                n_high, n_low = halves(tails[i, size + sides :])
                maps[i] = jnp.concatenate(
                    [jnp.concatenate([w_high, w_low], axis=1), jnp.concatenate([n_high, n_low], axis=1)],
                    axis=0,
                )

        @pl.when(side == 0)
        def _():
            more = product(jnp.concatenate([turned, second[n0:]], axis=0), fq[...])
            fs[...] = fs[...] + more[: size + sides]
            fq[...] = more[size + sides :]

        @pl.when(side == 1)
        def _():
            more = product(front, fp[:size])
            fp[size:] = fp[size:] + more[size:]
            fp[:size] = more[:size]
            more = product(front, fs[:size])
            fs[size:] = fs[size:] + more[size:]
            fs[:size] = more[:size]

    mine = group.at[depth, 0]

    def step_left(index):
        if index == 0:
            enter[...] = jnp.zeros((sides, size), jnp.float32)
            reach = mine[c0:w0]
        else:
            enter_right.wait_recv()
            reach = product(enter[...], mine[m0:c0]) + mine[c0:w0]
            enter_on[...] = reach
            enter_right.start()
        if index == planes // 2 - 1:
            if index > 0:
                partial = product(enter[...], mine[w0:b0]) + mine[b0:n0]
            met_left.wait_recv()
            leave[...] = product(reach, met[:size]) + met[size:]
        else:
            if index > 0:
                partial = product(enter[...], mine[w0:b0]) + mine[b0:n0]
            leave_left.wait_recv()
        if index > 0:
            leave_on[...] = product(leave[...], mine[n0:]) + partial
            leave_left.start()
            leave_left.wait_send()
        enter_right.wait_send()

    def step_right(index):
        if index < planes - 1:
            met_left.wait_recv()
            turned = product(mine[m0:w0], met[:size])
            turned = jnp.concatenate([turned[:size], turned[size:] + met[size:]], axis=0)
            met_on[...] = product(turned, mine[n0:]) + mine[w0:n0]
            met_left.start()
        enter_right.wait_recv()
        if index < planes - 1:
            reach = product(enter[...], mine[m0:c0]) + mine[c0:w0]
            enter_on[...] = reach
            enter_right.start()
            leave[...] = product(reach, met[:size]) + met[size:]
            enter_right.wait_send()
        else:
            leave[...] = jnp.zeros((sides, size), jnp.float32)
        met_left.wait_send()

    for index in range(planes):
        pl.when(plane == index)(functools.partial(step_left if index < planes // 2 else step_right, index))

    x_in = product(enter[...], fp[:size]) + fp[size:]
    y_in = product(leave[...], fq[...]) + product(enter[...], fs[:size]) + fs[size:]
    x_high, x_low = halves(x_in)
    y_high, y_low = halves(y_in)
    left = jnp.concatenate(
        [jnp.concatenate([x_high, y_high], axis=1), jnp.concatenate([x_low, y_low], axis=1)], axis=0
    )
    for i in range(rows):
        both = fold(jnp.dot(left, maps[i], preferred_element_type=jnp.float32), size)
        out[i] = tails[i, size : size + sides] + both[:sides] + both[sides:]


def on_device(levels, planes, rhs, pivot_inv, lower_gain, upper_gain):
    rows, sides, size = rhs.shape
    depth = len(levels)
    span = 3 * size + 2 * sides
    f32 = jnp.float32
    return pl.pallas_call(
        functools.partial(kernel, levels, planes),
        out_shape=jax.ShapeDtypeStruct(rhs.shape, f32),
        in_specs=[pl.BlockSpec(memory_space=pltpu.HBM)] * 4,
        out_specs=pl.BlockSpec(memory_space=pltpu.VMEM),
        scratch_shapes=[
            pltpu.VMEM((rows, sides, size), f32),
            pltpu.VMEM((rows, size, size), f32),
            pltpu.VMEM((rows, size, size), f32),
            pltpu.VMEM((rows, size, size), f32),
            pltpu.VMEM((rows, size + sides, size), f32),
            pltpu.VMEM((rows, 2 * size + sides, size), f32),
            pltpu.VMEM((rows, 2 * size, 2 * size), jnp.bfloat16),
            pltpu.VMEM((depth + 1, 2, span, size), f32),
            pltpu.VMEM((size + sides, size), f32),
            pltpu.VMEM((size, size), f32),
            pltpu.VMEM((size + sides, size), f32),
            pltpu.VMEM((sides, size), f32),
            pltpu.VMEM((sides, size), f32),
            pltpu.VMEM((size + sides, size), f32),
            pltpu.VMEM((sides, size), f32),
            pltpu.VMEM((sides, size), f32),
            pltpu.VMEM((size + sides, size), f32),
            pltpu.SemaphoreType.DMA((4, rows // PIECE)),
            pltpu.SemaphoreType.DMA((depth, PARTS)),
            pltpu.SemaphoreType.DMA((depth, PARTS)),
            pltpu.SemaphoreType.DMA((depth, PARTS)),
            pltpu.SemaphoreType.DMA((depth, PARTS)),
            pltpu.SemaphoreType.DMA((3,)),
            pltpu.SemaphoreType.DMA((3,)),
        ],
        compiler_params=pltpu.CompilerParams(
            collective_id=0, has_side_effects=True, vmem_limit_bytes=40 * 2**20
        ),
    )(rhs, pivot_inv, lower_gain, upper_gain)


def solution(mesh):
    levels = []
    planes = min(4, mesh.shape["wide"])
    for axis, count in (("narrow", mesh.shape["narrow"]), ("wide", mesh.shape["wide"] // planes)):
        stride = 1
        while stride < count:
            levels.append((axis, stride))
            stride *= 2
    placed = P(("wide", "narrow"), None, None)
    return jax.shard_map(
        functools.partial(on_device, tuple(levels), planes),
        mesh=mesh,
        in_specs=(placed,) * 4,
        out_specs=placed,
        check_vma=False,
    )
```

```python
import functools

import jax
import jax.numpy as jnp
from jax import lax
from jax.experimental import pallas as pl
from jax.experimental.pallas import tpu as pltpu
from jax.sharding import PartitionSpec as P

MESH = pl.DeviceIdType.MESH
SEGMENT = 3
PARTS = 2


def halves(value):
    high = value.astype(jnp.bfloat16)
    low = (value - high.astype(jnp.float32)).astype(jnp.bfloat16)
    return high, low


def right_side(value):
    high, low = halves(value)
    row = jnp.concatenate([high, low], axis=1)
    return jnp.concatenate([row, row], axis=0)


def left_side(value):
    high, low = halves(value)
    return jnp.concatenate([high, low], axis=1)


def fold(value, width):
    return value[:, :width] + value[:, width:]


def product(left, right):
    wide = jnp.dot(left_side(left), right_side(right), preferred_element_type=jnp.float32)
    return fold(wide, right.shape[1])


def kernel(
    levels,
    planes,
    rhs_hbm,
    pivot_hbm,
    lower_hbm,
    upper_hbm,
    out,
    rhs,
    pivot,
    lower,
    upper,
    ahead,
    tails,
    maps,
    seg_into,
    seg_leaves,
    seg_cross,
    group,
    fp,
    fq,
    fs,
    enter,
    leave,
    met,
    enter_on,
    leave_on,
    met_on,
    load_sem,
    send_sem,
    recv_sem,
    pass_send_sem,
    pass_recv_sem,
    chain_send_sem,
    chain_recv_sem,
):
    rows, sides, size = rhs.shape
    m0, c0, w0, b0, n0, end = 0, size, size + sides, 2 * size + sides, 2 * (size + sides), 3 * size + 2 * sides
    names = ("wide", "narrow")
    place = {name: lax.axis_index(name) for name in names}
    depth = len(levels)

    segments = rows // SEGMENT
    loads = []
    for kind, (source, target) in enumerate(
        ((rhs_hbm, rhs), (pivot_hbm, pivot), (lower_hbm, lower), (upper_hbm, upper))
    ):
        for piece in range(segments):
            span = pl.ds(piece * SEGMENT, SEGMENT)
            load = pltpu.make_async_copy(source.at[span], target.at[span], load_sem.at[kind, piece])
            load.start()
            loads.append(load)

    def partner(level):
        axis, stride = levels[level]
        mine = place[axis]
        side = lax.rem(lax.div(mine, stride), 2)
        other = mine + stride - 2 * stride * side
        return side, tuple(other if name == axis else place[name] for name in names)

    hop = lax.axis_size("wide") // planes
    plane = lax.div(place["wide"], hop)
    before = (place["wide"] - hop, place["narrow"])
    after = (place["wide"] + hop, place["narrow"])
    sibling = (place["wide"], 1 - place["narrow"])

    barrier = pltpu.get_barrier_semaphore()
    for level in range(depth):
        pl.semaphore_signal(barrier, inc=1, device_id=partner(level)[1], device_id_type=MESH)

    @pl.when(plane > 0)
    def _():
        pl.semaphore_signal(barrier, inc=1, device_id=before, device_id_type=MESH)

    @pl.when(plane < planes - 1)
    def _():
        pl.semaphore_signal(barrier, inc=1, device_id=after, device_id_type=MESH)

    for load in loads[: 2 * segments]:
        load.wait()
    for i in range(rows):
        ahead[i, size:] = product(rhs[i], pivot[i])
    for load in loads[2 * segments :]:
        load.wait()

    starts = [segment * SEGMENT for segment in range(segments)]
    fronts, backs = [], []
    for begin in starts:
        fronts.append(jnp.concatenate([-lower[begin], ahead[begin, size:]], axis=0))
        ahead[begin, :size] = fronts[-1][:size]
        backs.append(-upper[begin + SEGMENT - 1])
        tails[begin + SEGMENT - 1, size + sides :] = backs[-1]
    for k in range(1, SEGMENT):
        for s, begin in enumerate(starts):
            i, j = begin + k, begin + SEGMENT - 1 - k
            step = product(fronts[s], lower[i])
            fronts[s] = jnp.concatenate([-step[:size], ahead[i, size:] - step[size:]], axis=0)
            ahead[i] = fronts[s]
            backs[s] = -product(backs[s], upper[j])
            tails[j, size + sides :] = backs[s]
    totals = list(fronts)
    for s, begin in enumerate(starts):
        tails[begin + SEGMENT - 1, : size + sides] = totals[s]
    for k in range(1, SEGMENT):
        for s, begin in enumerate(starts):
            j = begin + SEGMENT - 1 - k
            totals[s] = ahead[j] - product(totals[s], upper[j])
            tails[j, : size + sides] = totals[s]

    def compose(front, first_total, first_back, second_front, second_total, second_back):
        joined = jnp.dot(
            left_side(front),
            jnp.concatenate([right_side(second_front[:size]), right_side(second_total[:size])], axis=1),
            preferred_element_type=jnp.float32,
        )
        onward = add_offset(fold(joined[:, : 2 * size], size), second_front[size:])
        turned = add_offset(fold(joined[:, 2 * size :], size), second_total[size:])
        turned = jnp.concatenate([turned, second_back], axis=0)
        returned = product(turned, first_back)
        return onward, first_total + returned[: size + sides], returned[size + sides :], turned

    def add_offset(value, offset):
        return jnp.concatenate([value[:size], value[size:] + offset], axis=0)

    spans = [(fronts[s], totals[s], backs[s]) for s in range(segments)]
    joins = []
    while len(spans) > 1:
        made = [compose(*spans[k], *spans[k + 1]) for k in range(0, len(spans), 2)]
        joins.append([(spans[2 * k][0], made[k][3]) for k in range(len(made))])
        spans = [one[:3] for one in made]
    local_front, local_total, local_back = spans[0]

    inner = (plane > 0).astype(jnp.int32) + (plane < planes - 1).astype(jnp.int32)
    pl.semaphore_wait(barrier, depth + inner)

    part = end // (2 * PARTS)

    def exchange(level):
        side, other = partner(level)
        if levels[level][0] == "narrow":
            spans = [pl.ds(0, end)]
        else:
            begin = place["narrow"] * (end // 2)
            spans = [pl.ds(pl.multiple_of(begin + k * part, part), part) for k in range(PARTS)]
        return [
            pltpu.make_async_remote_copy(
                src_ref=group.at[level, side, span],
                dst_ref=group.at[level, side, span],
                send_sem=send_sem.at[level, k],
                recv_sem=recv_sem.at[level, k],
                device_id=other,
                device_id_type=MESH,
            )
            for k, span in enumerate(spans)
        ]

    def finish(level, copies):
        if levels[level][0] == "narrow":
            copies[0].wait()
            return
        side = partner(level)[0]
        begin = place["narrow"] * (end // 2)
        relays = []
        for k, copy in enumerate(copies):
            copy.wait_recv()
            span = pl.ds(pl.multiple_of(begin + k * part, part), part)
            relay = pltpu.make_async_remote_copy(
                src_ref=group.at[level, 1 - side, span],
                dst_ref=group.at[level, 1 - side, span],
                send_sem=pass_send_sem.at[level, k],
                recv_sem=pass_recv_sem.at[level, k],
                device_id=sibling,
                device_id_type=MESH,
            )
            relay.start()
            relays.append(relay)
        for copy in copies:
            copy.wait_send()
        for relay in relays:
            relay.wait()

    side = partner(0)[0]
    group[0, side, m0:w0] = local_front
    group[0, side, w0:n0] = local_total
    group[0, side, n0:] = local_back
    copies = exchange(0)
    for copy in copies:
        copy.start()

    into, leaves, crosses = [None] * segments, [None] * segments, [None] * segments
    for level, pairs in enumerate(joins):
        for s in range(segments):
            front, turned = pairs[s >> (level + 1)]
            if (s >> level) & 1 == 0:
                if leaves[s] is None:
                    more = turned
                else:
                    more = product(turned, leaves[s])
                leaves[s] = more[size + sides :]
                cross = more[: size + sides]
                crosses[s] = cross if crosses[s] is None else crosses[s] + cross
            else:
                into[s] = front if into[s] is None else add_offset(product(front, into[s][:size]), into[s][size:])
                if crosses[s] is not None:
                    crosses[s] = add_offset(product(front, crosses[s][:size]), crosses[s][size:])
    has_into = [value is not None for value in into]
    has_leaves = [value is not None for value in leaves]
    has_cross = [value is not None for value in crosses]
    for s in range(segments):
        if has_into[s]:
            seg_into[s] = into[s]
        if has_leaves[s]:
            seg_leaves[s] = leaves[s]
        if has_cross[s]:
            seg_cross[s] = crosses[s]

    eye = (
        lax.broadcasted_iota(jnp.int32, (size, size), 0) == lax.broadcasted_iota(jnp.int32, (size, size), 1)
    ).astype(jnp.float32)
    fp[:size] = eye
    fp[size:] = jnp.zeros((sides, size), jnp.float32)
    fq[...] = eye
    fs[...] = jnp.zeros((size + sides, size), jnp.float32)

    def hand(kind, source, target, device):
        return pltpu.make_async_remote_copy(
            src_ref=source,
            dst_ref=target,
            send_sem=chain_send_sem.at[kind],
            recv_sem=chain_recv_sem.at[kind],
            device_id=device,
            device_id_type=MESH,
        )

    enter_right = hand(0, enter_on, enter, after)
    met_left = hand(1, met_on, met, before)
    leave_left = hand(2, leave_on, leave, before)

    for level in range(depth):
        finish(level, copies)
        side = partner(level)[0]
        first, second = group.at[level, 0], group.at[level, 1]
        front = first[m0:w0]
        onward, total, back, turned = compose(
            front, first[w0:n0], first[n0:], second[m0:w0], second[w0:n0], second[n0:]
        )
        following = partner(level + 1)[0] if level < depth - 1 else 0
        group[level + 1, following, m0:w0] = onward
        group[level + 1, following, w0:n0] = total
        group[level + 1, following, n0:] = back
        if level < depth - 1:
            copies = exchange(level + 1)
            for copy in copies:
                copy.start()
        else:

            @pl.when(plane == 0)
            def _():
                enter_on[...] = group[depth, 0, c0:w0]
                enter_right.start()

            @pl.when(plane == planes - 1)
            def _():
                met_on[...] = group[depth, 0, w0:n0]
                met_left.start()

        if level == 0:
            for i in range(rows):
                w_high, w_low = halves(tails[i, :size])
                n_high, n_low = halves(tails[i, size + sides :])
                maps[i] = jnp.concatenate(
                    [jnp.concatenate([w_high, w_low], axis=1), jnp.concatenate([n_high, n_low], axis=1)],
                    axis=0,
                )

        @pl.when(side == 0)
        def _():
            more = product(turned, fq[...])
            fs[...] = fs[...] + more[: size + sides]
            fq[...] = more[size + sides :]

        @pl.when(side == 1)
        def _():
            more = product(front, fp[:size])
            fp[size:] = fp[size:] + more[size:]
            fp[:size] = more[:size]
            more = product(front, fs[:size])
            fs[size:] = fs[size:] + more[size:]
            fs[:size] = more[:size]

    mine = group.at[depth, 0]

    def step_left(index):
        if index == 0:
            enter[...] = jnp.zeros((sides, size), jnp.float32)
            reach = mine[c0:w0]
        else:
            enter_right.wait_recv()
            reach = product(enter[...], mine[m0:c0]) + mine[c0:w0]
            enter_on[...] = reach
            enter_right.start()
        if index == planes // 2 - 1:
            if index > 0:
                partial = product(enter[...], mine[w0:b0]) + mine[b0:n0]
            met_left.wait_recv()
            leave[...] = product(reach, met[:size]) + met[size:]
        else:
            if index > 0:
                partial = product(enter[...], mine[w0:b0]) + mine[b0:n0]
            leave_left.wait_recv()
        if index > 0:
            leave_on[...] = product(leave[...], mine[n0:]) + partial
            leave_left.start()
            leave_left.wait_send()
        enter_right.wait_send()

    def step_right(index):
        if index < planes - 1:
            met_left.wait_recv()
            turned = product(mine[m0:w0], met[:size])
            turned = jnp.concatenate([turned[:size], turned[size:] + met[size:]], axis=0)
            met_on[...] = product(turned, mine[n0:]) + mine[w0:n0]
            met_left.start()
        enter_right.wait_recv()
        if index < planes - 1:
            reach = product(enter[...], mine[m0:c0]) + mine[c0:w0]
            enter_on[...] = reach
            enter_right.start()
            leave[...] = product(reach, met[:size]) + met[size:]
            enter_right.wait_send()
        else:
            leave[...] = jnp.zeros((sides, size), jnp.float32)
        met_left.wait_send()

    for index in range(planes):
        pl.when(plane == index)(functools.partial(step_left if index < planes // 2 else step_right, index))

    x_in = product(enter[...], fp[:size]) + fp[size:]
    y_in = product(leave[...], fq[...]) + product(enter[...], fs[:size]) + fs[size:]
    for s, begin in enumerate(starts):
        x_here, y_here = x_in, y_in
        if has_into[s]:
            x_here = product(x_in, seg_into[s, :size]) + seg_into[s, size:]
        if has_leaves[s]:
            y_here = product(y_in, seg_leaves[s])
        if has_cross[s]:
            y_here = y_here + product(x_in, seg_cross[s, :size]) + seg_cross[s, size:]
        x_high, x_low = halves(x_here)
        y_high, y_low = halves(y_here)
        left = jnp.concatenate(
            [jnp.concatenate([x_high, y_high], axis=1), jnp.concatenate([x_low, y_low], axis=1)], axis=0
        )
        for i in range(begin, begin + SEGMENT):
            both = fold(jnp.dot(left, maps[i], preferred_element_type=jnp.float32), size)
            out[i] = tails[i, size : size + sides] + both[:sides] + both[sides:]


def on_device(levels, planes, rhs, pivot_inv, lower_gain, upper_gain):
    rows, sides, size = rhs.shape
    depth = len(levels)
    span = 3 * size + 2 * sides
    f32 = jnp.float32
    return pl.pallas_call(
        functools.partial(kernel, levels, planes),
        out_shape=jax.ShapeDtypeStruct(rhs.shape, f32),
        in_specs=[pl.BlockSpec(memory_space=pltpu.HBM)] * 4,
        out_specs=pl.BlockSpec(memory_space=pltpu.VMEM),
        scratch_shapes=[
            pltpu.VMEM((rows, sides, size), f32),
            pltpu.VMEM((rows, size, size), f32),
            pltpu.VMEM((rows, size, size), f32),
            pltpu.VMEM((rows, size, size), f32),
            pltpu.VMEM((rows, size + sides, size), f32),
            pltpu.VMEM((rows, 2 * size + sides, size), f32),
            pltpu.VMEM((rows, 2 * size, 2 * size), jnp.bfloat16),
            pltpu.VMEM((rows // SEGMENT, size + sides, size), f32),
            pltpu.VMEM((rows // SEGMENT, size, size), f32),
            pltpu.VMEM((rows // SEGMENT, size + sides, size), f32),
            pltpu.VMEM((depth + 1, 2, span, size), f32),
            pltpu.VMEM((size + sides, size), f32),
            pltpu.VMEM((size, size), f32),
            pltpu.VMEM((size + sides, size), f32),
            pltpu.VMEM((sides, size), f32),
            pltpu.VMEM((sides, size), f32),
            pltpu.VMEM((size + sides, size), f32),
            pltpu.VMEM((sides, size), f32),
            pltpu.VMEM((sides, size), f32),
            pltpu.VMEM((size + sides, size), f32),
            pltpu.SemaphoreType.DMA((4, rows // SEGMENT)),
            pltpu.SemaphoreType.DMA((depth, PARTS)),
            pltpu.SemaphoreType.DMA((depth, PARTS)),
            pltpu.SemaphoreType.DMA((depth, PARTS)),
            pltpu.SemaphoreType.DMA((depth, PARTS)),
            pltpu.SemaphoreType.DMA((3,)),
            pltpu.SemaphoreType.DMA((3,)),
        ],
        compiler_params=pltpu.CompilerParams(
            collective_id=0, has_side_effects=True, vmem_limit_bytes=63 * 2**20
        ),
    )(rhs, pivot_inv, lower_gain, upper_gain)


def solution(mesh):
    levels = []
    planes = min(4, mesh.shape["wide"])
    for axis, count in (("narrow", mesh.shape["narrow"]), ("wide", mesh.shape["wide"] // planes)):
        stride = 1
        while stride < count:
            levels.append((axis, stride))
            stride *= 2
    placed = P(("wide", "narrow"), None, None)
    return jax.shard_map(
        functools.partial(on_device, tuple(levels), planes),
        mesh=mesh,
        in_specs=(placed,) * 4,
        out_specs=placed,
        check_vma=False,
    )
```

```python
import functools

import jax
import jax.numpy as jnp
from jax import lax
from jax.experimental import pallas as pl
from jax.experimental.pallas import tpu as pltpu
from jax.sharding import PartitionSpec as P

MESH = pl.DeviceIdType.MESH
SEGMENT = 3
PARTS = 2


def halves(value):
    high = value.astype(jnp.bfloat16)
    low = (value - high.astype(jnp.float32)).astype(jnp.bfloat16)
    return high, low


def right_side(value):
    high, low = halves(value)
    row = jnp.concatenate([high, low], axis=1)
    return jnp.concatenate([row, row], axis=0)


def left_side(value):
    high, low = halves(value)
    return jnp.concatenate([high, low], axis=1)


def fold(value, width):
    return value[:, :width] + value[:, width:]


def product(left, right):
    wide = jnp.dot(left_side(left), right_side(right), preferred_element_type=jnp.float32)
    return fold(wide, right.shape[1])


def kernel(
    levels,
    planes,
    rhs_hbm,
    pivot_hbm,
    lower_hbm,
    upper_hbm,
    out,
    rhs,
    pivot,
    lower,
    upper,
    ahead,
    tails,
    maps,
    seg_into,
    seg_leaves,
    seg_cross,
    group,
    fp,
    fq,
    fs,
    enter,
    leave,
    met,
    enter_on,
    leave_on,
    met_on,
    load_sem,
    send_sem,
    recv_sem,
    pass_send_sem,
    pass_recv_sem,
    chain_send_sem,
    chain_recv_sem,
):
    rows, sides, size = rhs.shape
    m0, c0, w0, b0, n0, end = 0, size, size + sides, 2 * size + sides, 2 * (size + sides), 3 * size + 2 * sides
    names = ("wide", "narrow")
    place = {name: lax.axis_index(name) for name in names}
    depth = len(levels)

    segments = rows // SEGMENT
    loads = []
    for kind, (source, target) in enumerate(
        ((rhs_hbm, rhs), (pivot_hbm, pivot), (lower_hbm, lower), (upper_hbm, upper))
    ):
        for piece in range(segments):
            span = pl.ds(piece * SEGMENT, SEGMENT)
            load = pltpu.make_async_copy(source.at[span], target.at[span], load_sem.at[kind, piece])
            load.start()
            loads.append(load)

    def partner(level):
        axis, stride = levels[level]
        mine = place[axis]
        side = lax.rem(lax.div(mine, stride), 2)
        other = mine + stride - 2 * stride * side
        return side, tuple(other if name == axis else place[name] for name in names)

    hop = lax.axis_size("wide") // planes
    plane = lax.div(place["wide"], hop)
    before = (place["wide"] - hop, place["narrow"])
    after = (place["wide"] + hop, place["narrow"])
    sibling = (place["wide"], 1 - place["narrow"])

    barrier = pltpu.get_barrier_semaphore()
    for level in range(depth):
        pl.semaphore_signal(barrier, inc=1, device_id=partner(level)[1], device_id_type=MESH)

    @pl.when(plane > 0)
    def _():
        pl.semaphore_signal(barrier, inc=1, device_id=before, device_id_type=MESH)

    @pl.when(plane < planes - 1)
    def _():
        pl.semaphore_signal(barrier, inc=1, device_id=after, device_id_type=MESH)

    for load in loads[: 2 * segments]:
        load.wait()
    for i in range(rows):
        ahead[i, size:] = product(rhs[i], pivot[i])
    for load in loads[2 * segments :]:
        load.wait()

    starts = [segment * SEGMENT for segment in range(segments)]
    fronts, backs = [], []
    for begin in starts:
        fronts.append(jnp.concatenate([-lower[begin], ahead[begin, size:]], axis=0))
        ahead[begin, :size] = fronts[-1][:size]
        backs.append(-upper[begin + SEGMENT - 1])
        tails[begin + SEGMENT - 1, size + sides :] = backs[-1]
    for k in range(1, SEGMENT):
        for s, begin in enumerate(starts):
            i, j = begin + k, begin + SEGMENT - 1 - k
            step = product(fronts[s], lower[i])
            fronts[s] = jnp.concatenate([-step[:size], ahead[i, size:] - step[size:]], axis=0)
            ahead[i] = fronts[s]
            backs[s] = -product(backs[s], upper[j])
            tails[j, size + sides :] = backs[s]
    totals = list(fronts)
    for s, begin in enumerate(starts):
        tails[begin + SEGMENT - 1, : size + sides] = totals[s]
    for k in range(1, SEGMENT):
        for s, begin in enumerate(starts):
            j = begin + SEGMENT - 1 - k
            totals[s] = ahead[j] - product(totals[s], upper[j])
            tails[j, : size + sides] = totals[s]

    def compose(front, first_total, first_back, second_front, second_total, second_back):
        joined = jnp.dot(
            left_side(front),
            jnp.concatenate([right_side(second_front[:size]), right_side(second_total[:size])], axis=1),
            preferred_element_type=jnp.float32,
        )
        onward = add_offset(fold(joined[:, : 2 * size], size), second_front[size:])
        turned = add_offset(fold(joined[:, 2 * size :], size), second_total[size:])
        turned = jnp.concatenate([turned, second_back], axis=0)
        returned = product(turned, first_back)
        return onward, first_total + returned[: size + sides], returned[size + sides :], turned

    def add_offset(value, offset):
        return jnp.concatenate([value[:size], value[size:] + offset], axis=0)

    spans = [(fronts[s], totals[s], backs[s]) for s in range(segments)]
    joins = []
    while len(spans) > 1:
        made = [compose(*spans[k], *spans[k + 1]) for k in range(0, len(spans), 2)]
        joins.append([(spans[2 * k][0], made[k][3]) for k in range(len(made))])
        spans = [one[:3] for one in made]
    local_front, local_total, local_back = spans[0]

    inner = (plane > 0).astype(jnp.int32) + (plane < planes - 1).astype(jnp.int32)
    pl.semaphore_wait(barrier, depth + inner)

    part = end // (2 * PARTS)

    def exchange(level):
        side, other = partner(level)
        if levels[level][0] == "narrow":
            spans = [pl.ds(0, end)]
        else:
            begin = place["narrow"] * (end // 2)
            spans = [pl.ds(pl.multiple_of(begin + k * part, part), part) for k in range(PARTS)]
        return [
            pltpu.make_async_remote_copy(
                src_ref=group.at[level, side, span],
                dst_ref=group.at[level, side, span],
                send_sem=send_sem.at[level, k],
                recv_sem=recv_sem.at[level, k],
                device_id=other,
                device_id_type=MESH,
            )
            for k, span in enumerate(spans)
        ]

    def finish(level, copies):
        if levels[level][0] == "narrow":
            copies[0].wait()
            return
        side = partner(level)[0]
        begin = place["narrow"] * (end // 2)
        relays = []
        for k, copy in enumerate(copies):
            copy.wait_recv()
            span = pl.ds(pl.multiple_of(begin + k * part, part), part)
            relay = pltpu.make_async_remote_copy(
                src_ref=group.at[level, 1 - side, span],
                dst_ref=group.at[level, 1 - side, span],
                send_sem=pass_send_sem.at[level, k],
                recv_sem=pass_recv_sem.at[level, k],
                device_id=sibling,
                device_id_type=MESH,
            )
            relay.start()
            relays.append(relay)
        for copy in copies:
            copy.wait_send()
        for relay in relays:
            relay.wait()

    side = partner(0)[0]
    group[0, side, m0:w0] = local_front
    group[0, side, w0:n0] = local_total
    group[0, side, n0:] = local_back
    copies = exchange(0)
    for copy in copies:
        copy.start()

    into, leaves, crosses = [None] * segments, [None] * segments, [None] * segments
    for level, pairs in enumerate(joins):
        for s in range(segments):
            front, turned = pairs[s >> (level + 1)]
            if (s >> level) & 1 == 0:
                if leaves[s] is None:
                    more = turned
                else:
                    more = product(turned, leaves[s])
                leaves[s] = more[size + sides :]
                cross = more[: size + sides]
                crosses[s] = cross if crosses[s] is None else crosses[s] + cross
            else:
                into[s] = front if into[s] is None else add_offset(product(front, into[s][:size]), into[s][size:])
                if crosses[s] is not None:
                    crosses[s] = add_offset(product(front, crosses[s][:size]), crosses[s][size:])
    has_into = [value is not None for value in into]
    has_leaves = [value is not None for value in leaves]
    has_cross = [value is not None for value in crosses]
    for s in range(segments):
        if has_into[s]:
            seg_into[s] = into[s]
        if has_leaves[s]:
            seg_leaves[s] = leaves[s]
        if has_cross[s]:
            seg_cross[s] = crosses[s]

    eye = (
        lax.broadcasted_iota(jnp.int32, (size, size), 0) == lax.broadcasted_iota(jnp.int32, (size, size), 1)
    ).astype(jnp.float32)
    fp[:size] = eye
    fp[size:] = jnp.zeros((sides, size), jnp.float32)
    fq[...] = eye
    fs[...] = jnp.zeros((size + sides, size), jnp.float32)

    def hand(kind, source, target, device):
        return pltpu.make_async_remote_copy(
            src_ref=source,
            dst_ref=target,
            send_sem=chain_send_sem.at[kind],
            recv_sem=chain_recv_sem.at[kind],
            device_id=device,
            device_id_type=MESH,
        )

    enter_right = hand(0, enter_on, enter, after)
    met_left = hand(1, met_on, met, before)
    leave_left = hand(2, leave_on, leave, before)

    for level in range(depth):
        finish(level, copies)
        side = partner(level)[0]
        first, second = group.at[level, 0], group.at[level, 1]
        front = first[m0:w0]
        onward, total, back, turned = compose(
            front, first[w0:n0], first[n0:], second[m0:w0], second[w0:n0], second[n0:]
        )
        following = partner(level + 1)[0] if level < depth - 1 else 0
        group[level + 1, following, m0:w0] = onward
        group[level + 1, following, w0:n0] = total
        group[level + 1, following, n0:] = back
        if level < depth - 1:
            copies = exchange(level + 1)
            for copy in copies:
                copy.start()
        else:

            @pl.when(plane == 0)
            def _():
                enter_on[...] = group[depth, 0, c0:w0]
                enter_right.start()

            @pl.when(plane == planes - 1)
            def _():
                met_on[...] = group[depth, 0, w0:n0]
                met_left.start()

        if level == 0:
            for i in range(rows):
                w_high, w_low = halves(tails[i, :size])
                n_high, n_low = halves(tails[i, size + sides :])
                maps[i] = jnp.concatenate(
                    [jnp.concatenate([w_high, w_low], axis=1), jnp.concatenate([n_high, n_low], axis=1)],
                    axis=0,
                )

        @pl.when(side == 0)
        def _():
            more = product(turned, fq[...])
            fs[...] = fs[...] + more[: size + sides]
            fq[...] = more[size + sides :]

        @pl.when(side == 1)
        def _():
            more = product(front, fp[:size])
            fp[size:] = fp[size:] + more[size:]
            fp[:size] = more[:size]
            more = product(front, fs[:size])
            fs[size:] = fs[size:] + more[size:]
            fs[:size] = more[:size]

    mine = group.at[depth, 0]

    def step_left(index):
        if index == 0:
            enter[...] = jnp.zeros((sides, size), jnp.float32)
            reach = mine[c0:w0]
        else:
            enter_right.wait_recv()
            reach = product(enter[...], mine[m0:c0]) + mine[c0:w0]
            enter_on[...] = reach
            enter_right.start()
        if index == planes - 2:
            if index > 0:
                partial = product(enter[...], mine[w0:b0]) + mine[b0:n0]
            met_left.wait_recv()
            leave[...] = product(reach, met[:size]) + met[size:]
        else:
            if index > 0:
                partial = product(enter[...], mine[w0:b0]) + mine[b0:n0]
            leave_left.wait_recv()
        if index > 0:
            leave_on[...] = product(leave[...], mine[n0:]) + partial
            leave_left.start()
            leave_left.wait_send()
        enter_right.wait_send()

    def step_right(index):
        if index < planes - 1:
            met_left.wait_recv()
            turned = product(mine[m0:w0], met[:size])
            turned = jnp.concatenate([turned[:size], turned[size:] + met[size:]], axis=0)
            met_on[...] = product(turned, mine[n0:]) + mine[w0:n0]
            met_left.start()
        enter_right.wait_recv()
        if index < planes - 1:
            reach = product(enter[...], mine[m0:c0]) + mine[c0:w0]
            enter_on[...] = reach
            enter_right.start()
            leave[...] = product(reach, met[:size]) + met[size:]
            enter_right.wait_send()
        else:
            leave[...] = jnp.zeros((sides, size), jnp.float32)
        met_left.wait_send()

    for index in range(planes):
        pl.when(plane == index)(functools.partial(step_left if index < planes - 1 else step_right, index))

    x_in = product(enter[...], fp[:size]) + fp[size:]
    y_in = product(leave[...], fq[...]) + product(enter[...], fs[:size]) + fs[size:]
    for s, begin in enumerate(starts):
        x_here, y_here = x_in, y_in
        if has_into[s]:
            x_here = product(x_in, seg_into[s, :size]) + seg_into[s, size:]
        if has_leaves[s]:
            y_here = product(y_in, seg_leaves[s])
        if has_cross[s]:
            y_here = y_here + product(x_in, seg_cross[s, :size]) + seg_cross[s, size:]
        x_high, x_low = halves(x_here)
        y_high, y_low = halves(y_here)
        left = jnp.concatenate(
            [jnp.concatenate([x_high, y_high], axis=1), jnp.concatenate([x_low, y_low], axis=1)], axis=0
        )
        for i in range(begin, begin + SEGMENT):
            both = fold(jnp.dot(left, maps[i], preferred_element_type=jnp.float32), size)
            out[i] = tails[i, size : size + sides] + both[:sides] + both[sides:]


def on_device(levels, planes, rhs, pivot_inv, lower_gain, upper_gain):
    rows, sides, size = rhs.shape
    depth = len(levels)
    span = 3 * size + 2 * sides
    f32 = jnp.float32
    return pl.pallas_call(
        functools.partial(kernel, levels, planes),
        out_shape=pltpu.VMEM(rhs.shape, f32),
        in_specs=[pl.BlockSpec(memory_space=pltpu.HBM)] * 4,
        out_specs=pl.BlockSpec(memory_space=pltpu.VMEM),
        scratch_shapes=[
            pltpu.VMEM((rows, sides, size), f32),
            pltpu.VMEM((rows, size, size), f32),
            pltpu.VMEM((rows, size, size), f32),
            pltpu.VMEM((rows, size, size), f32),
            pltpu.VMEM((rows, size + sides, size), f32),
            pltpu.VMEM((rows, 2 * size + sides, size), f32),
            pltpu.VMEM((rows, 2 * size, 2 * size), jnp.bfloat16),
            pltpu.VMEM((rows // SEGMENT, size + sides, size), f32),
            pltpu.VMEM((rows // SEGMENT, size, size), f32),
            pltpu.VMEM((rows // SEGMENT, size + sides, size), f32),
            pltpu.VMEM((depth + 1, 2, span, size), f32),
            pltpu.VMEM((size + sides, size), f32),
            pltpu.VMEM((size, size), f32),
            pltpu.VMEM((size + sides, size), f32),
            pltpu.VMEM((sides, size), f32),
            pltpu.VMEM((sides, size), f32),
            pltpu.VMEM((size + sides, size), f32),
            pltpu.VMEM((sides, size), f32),
            pltpu.VMEM((sides, size), f32),
            pltpu.VMEM((size + sides, size), f32),
            pltpu.SemaphoreType.DMA((4, rows // SEGMENT)),
            pltpu.SemaphoreType.DMA((depth, PARTS)),
            pltpu.SemaphoreType.DMA((depth, PARTS)),
            pltpu.SemaphoreType.DMA((depth, PARTS)),
            pltpu.SemaphoreType.DMA((depth, PARTS)),
            pltpu.SemaphoreType.DMA((3,)),
            pltpu.SemaphoreType.DMA((3,)),
        ],
        compiler_params=pltpu.CompilerParams(
            collective_id=0, has_side_effects=True, vmem_limit_bytes=62 * 2**20
        ),
    )(rhs, pivot_inv, lower_gain, upper_gain)


def solution(mesh):
    levels = []
    planes = min(4, mesh.shape["wide"])
    for axis, count in (("narrow", mesh.shape["narrow"]), ("wide", mesh.shape["wide"] // planes)):
        stride = 1
        while stride < count:
            levels.append((axis, stride))
            stride *= 2
    placed = P(("wide", "narrow"), None, None)
    return jax.shard_map(
        functools.partial(on_device, tuple(levels), planes),
        mesh=mesh,
        in_specs=(placed,) * 4,
        out_specs=placed,
        check_vma=False,
    )
```

```python
import functools

import jax
import jax.numpy as jnp
from jax import lax
from jax.experimental import pallas as pl
from jax.experimental.pallas import tpu as pltpu
from jax.sharding import PartitionSpec as P

MESH = pl.DeviceIdType.MESH
SEGMENT = 3
PARTS = 2


def halves(value):
    high = value.astype(jnp.bfloat16)
    low = (value - high.astype(jnp.float32)).astype(jnp.bfloat16)
    return high, low


def right_side(value):
    high, low = halves(value)
    row = jnp.concatenate([high, low], axis=1)
    return jnp.concatenate([row, row], axis=0)


def left_side(value):
    high, low = halves(value)
    return jnp.concatenate([high, low], axis=1)


def fold(value, width):
    return value[:, :width] + value[:, width:]


def product(left, right):
    wide = jnp.dot(left_side(left), right_side(right), preferred_element_type=jnp.float32)
    return fold(wide, right.shape[1])


def kernel(
    levels,
    planes,
    rhs_hbm,
    pivot_hbm,
    lower_hbm,
    upper_hbm,
    out,
    rhs,
    pivot,
    lower,
    upper,
    ahead,
    tails,
    maps,
    seg_into,
    seg_leaves,
    seg_cross,
    y_parts,
    y_maps,
    group,
    fp,
    fq,
    fs,
    enter,
    leave,
    met,
    enter_on,
    leave_on,
    met_on,
    load_sem,
    send_sem,
    recv_sem,
    pass_send_sem,
    pass_recv_sem,
    chain_send_sem,
    chain_recv_sem,
):
    rows, sides, size = rhs.shape
    m0, c0, w0, b0, n0, end = 0, size, size + sides, 2 * size + sides, 2 * (size + sides), 3 * size + 2 * sides
    names = ("wide", "narrow")
    place = {name: lax.axis_index(name) for name in names}
    depth = len(levels)

    segments = rows // SEGMENT
    loads = []
    for kind, (source, target) in enumerate(
        ((rhs_hbm, rhs), (pivot_hbm, pivot), (lower_hbm, lower), (upper_hbm, upper))
    ):
        for piece in range(segments):
            span = pl.ds(piece * SEGMENT, SEGMENT)
            load = pltpu.make_async_copy(source.at[span], target.at[span], load_sem.at[kind, piece])
            load.start()
            loads.append(load)

    def partner(level):
        axis, stride = levels[level]
        mine = place[axis]
        side = lax.rem(lax.div(mine, stride), 2)
        other = mine + stride - 2 * stride * side
        return side, tuple(other if name == axis else place[name] for name in names)

    hop = lax.axis_size("wide") // planes
    plane = lax.div(place["wide"], hop)
    before = (place["wide"] - hop, place["narrow"])
    after = (place["wide"] + hop, place["narrow"])
    sibling = (place["wide"], 1 - place["narrow"])

    barrier = pltpu.get_barrier_semaphore()
    for level in range(depth):
        pl.semaphore_signal(barrier, inc=1, device_id=partner(level)[1], device_id_type=MESH)

    @pl.when(plane > 0)
    def _():
        pl.semaphore_signal(barrier, inc=1, device_id=before, device_id_type=MESH)

    @pl.when(plane < planes - 1)
    def _():
        pl.semaphore_signal(barrier, inc=1, device_id=after, device_id_type=MESH)

    for load in loads[: 2 * segments]:
        load.wait()
    for i in range(rows):
        ahead[i, size:] = product(rhs[i], pivot[i])
    for load in loads[2 * segments :]:
        load.wait()

    starts = [segment * SEGMENT for segment in range(segments)]
    fronts, backs = [], []
    for begin in starts:
        fronts.append(jnp.concatenate([-lower[begin], ahead[begin, size:]], axis=0))
        ahead[begin, :size] = fronts[-1][:size]
        backs.append(-upper[begin + SEGMENT - 1])
        tails[begin + SEGMENT - 1, size + sides :] = backs[-1]
    for k in range(1, SEGMENT):
        for s, begin in enumerate(starts):
            i, j = begin + k, begin + SEGMENT - 1 - k
            step = product(fronts[s], lower[i])
            fronts[s] = jnp.concatenate([-step[:size], ahead[i, size:] - step[size:]], axis=0)
            ahead[i] = fronts[s]
            backs[s] = -product(backs[s], upper[j])
            tails[j, size + sides :] = backs[s]
    totals = list(fronts)
    for s, begin in enumerate(starts):
        tails[begin + SEGMENT - 1, : size + sides] = totals[s]
    for k in range(1, SEGMENT):
        for s, begin in enumerate(starts):
            j = begin + SEGMENT - 1 - k
            totals[s] = ahead[j] - product(totals[s], upper[j])
            tails[j, : size + sides] = totals[s]

    def compose(front, first_total, first_back, second_front, second_total, second_back):
        joined = jnp.dot(
            left_side(front),
            jnp.concatenate([right_side(second_front[:size]), right_side(second_total[:size])], axis=1),
            preferred_element_type=jnp.float32,
        )
        onward = add_offset(fold(joined[:, : 2 * size], size), second_front[size:])
        turned = add_offset(fold(joined[:, 2 * size :], size), second_total[size:])
        turned = jnp.concatenate([turned, second_back], axis=0)
        returned = product(turned, first_back)
        return onward, first_total + returned[: size + sides], returned[size + sides :], turned

    def add_offset(value, offset):
        return jnp.concatenate([value[:size], value[size:] + offset], axis=0)

    spans = [(fronts[s], totals[s], backs[s]) for s in range(segments)]
    joins = []
    while len(spans) > 1:
        made = [compose(*spans[k], *spans[k + 1]) for k in range(0, len(spans), 2)]
        joins.append([(spans[2 * k][0], made[k][3]) for k in range(len(made))])
        spans = [one[:3] for one in made]
    local_front, local_total, local_back = spans[0]

    inner = (plane > 0).astype(jnp.int32) + (plane < planes - 1).astype(jnp.int32)
    pl.semaphore_wait(barrier, depth + inner)

    part = end // (2 * PARTS)

    def exchange(level):
        side, other = partner(level)
        if levels[level][0] == "narrow":
            spans = [pl.ds(0, end)]
        else:
            begin = place["narrow"] * (end // 2)
            spans = [pl.ds(pl.multiple_of(begin + k * part, part), part) for k in range(PARTS)]
        return [
            pltpu.make_async_remote_copy(
                src_ref=group.at[level, side, span],
                dst_ref=group.at[level, side, span],
                send_sem=send_sem.at[level, k],
                recv_sem=recv_sem.at[level, k],
                device_id=other,
                device_id_type=MESH,
            )
            for k, span in enumerate(spans)
        ]

    def finish(level, copies):
        if levels[level][0] == "narrow":
            copies[0].wait()
            return
        side = partner(level)[0]
        begin = place["narrow"] * (end // 2)
        relays = []
        for k, copy in enumerate(copies):
            copy.wait_recv()
            span = pl.ds(pl.multiple_of(begin + k * part, part), part)
            relay = pltpu.make_async_remote_copy(
                src_ref=group.at[level, 1 - side, span],
                dst_ref=group.at[level, 1 - side, span],
                send_sem=pass_send_sem.at[level, k],
                recv_sem=pass_recv_sem.at[level, k],
                device_id=sibling,
                device_id_type=MESH,
            )
            relay.start()
            relays.append(relay)
        for copy in copies:
            copy.wait_send()
        for relay in relays:
            relay.wait()

    side = partner(0)[0]
    group[0, side, m0:w0] = local_front
    group[0, side, w0:n0] = local_total
    group[0, side, n0:] = local_back
    copies = exchange(0)
    for copy in copies:
        copy.start()

    into, leaves, crosses = [None] * segments, [None] * segments, [None] * segments
    for level, pairs in enumerate(joins):
        for s in range(segments):
            front, turned = pairs[s >> (level + 1)]
            if (s >> level) & 1 == 0:
                if leaves[s] is None:
                    more = turned
                else:
                    more = product(turned, leaves[s])
                leaves[s] = more[size + sides :]
                cross = more[: size + sides]
                crosses[s] = cross if crosses[s] is None else crosses[s] + cross
            else:
                into[s] = front if into[s] is None else add_offset(product(front, into[s][:size]), into[s][size:])
                if crosses[s] is not None:
                    crosses[s] = add_offset(product(front, crosses[s][:size]), crosses[s][size:])
    has_into = [value is not None for value in into]
    has_leaves = [value is not None for value in leaves]
    has_cross = [value is not None for value in crosses]
    for s in range(segments):
        if has_into[s]:
            seg_into[s] = into[s]
        if has_leaves[s]:
            seg_leaves[s] = leaves[s]
        if has_cross[s]:
            seg_cross[s] = crosses[s]

    eye = (
        lax.broadcasted_iota(jnp.int32, (size, size), 0) == lax.broadcasted_iota(jnp.int32, (size, size), 1)
    ).astype(jnp.float32)
    fp[:size] = eye
    fp[size:] = jnp.zeros((sides, size), jnp.float32)
    fq[...] = eye
    fs[...] = jnp.zeros((size + sides, size), jnp.float32)

    def hand(kind, source, target, device):
        return pltpu.make_async_remote_copy(
            src_ref=source,
            dst_ref=target,
            send_sem=chain_send_sem.at[kind],
            recv_sem=chain_recv_sem.at[kind],
            device_id=device,
            device_id_type=MESH,
        )

    enter_right = hand(0, enter_on, enter, after)
    met_left = hand(1, met_on, met, before)
    leave_left = hand(2, leave_on, leave, before)

    for level in range(depth):
        finish(level, copies)
        side = partner(level)[0]
        first, second = group.at[level, 0], group.at[level, 1]
        front = first[m0:w0]
        onward, total, back, turned = compose(
            front, first[w0:n0], first[n0:], second[m0:w0], second[w0:n0], second[n0:]
        )
        following = partner(level + 1)[0] if level < depth - 1 else 0
        group[level + 1, following, m0:w0] = onward
        group[level + 1, following, w0:n0] = total
        group[level + 1, following, n0:] = back
        if level < depth - 1:
            copies = exchange(level + 1)
            for copy in copies:
                copy.start()
        else:

            @pl.when(plane == 0)
            def _():
                enter_on[...] = group[depth, 0, c0:w0]
                enter_right.start()

            @pl.when(plane == planes - 1)
            def _():
                met_on[...] = group[depth, 0, w0:n0]
                met_left.start()

        if level == 0:
            for i in range(rows):
                maps[0, i] = right_side(tails[i, :size])
                maps[1, i] = right_side(tails[i, size + sides :])

        @pl.when(side == 0)
        def _():
            more = product(turned, fq[...])
            fs[...] = fs[...] + more[: size + sides]
            fq[...] = more[size + sides :]

        @pl.when(side == 1)
        def _():
            more = product(front, fp[:size])
            fp[size:] = fp[size:] + more[size:]
            fp[:size] = more[:size]
            more = product(front, fs[:size])
            fs[size:] = fs[size:] + more[size:]
            fs[:size] = more[:size]

    def prepare():
        x_in = product(enter[...], fp[:size]) + fp[size:]
        y_part = product(enter[...], fs[:size]) + fs[size:]
        for s, begin in enumerate(starts):
            x_here = x_in
            if has_into[s]:
                x_here = product(x_in, seg_into[s, :size]) + seg_into[s, size:]
            y_here = y_part
            back = fq[...]
            if has_leaves[s]:
                both = product(jnp.concatenate([y_part, back], axis=0), seg_leaves[s])
                y_here, back = both[:sides], both[sides:]
            if has_cross[s]:
                y_here = y_here + product(x_in, seg_cross[s, :size]) + seg_cross[s, size:]
            y_parts[s] = y_here
            y_maps[s] = right_side(back)
            left = left_side(x_here)
            for i in range(begin, begin + SEGMENT):
                more = jnp.dot(left, maps[0, i], preferred_element_type=jnp.float32)
                tails[i, size : size + sides] = tails[i, size : size + sides] + fold(more, size)

    mine = group.at[depth, 0]

    def step_left(index):
        if index == 0:
            enter[...] = jnp.zeros((sides, size), jnp.float32)
            reach = mine[c0:w0]
        else:
            enter_right.wait_recv()
            reach = product(enter[...], mine[m0:c0]) + mine[c0:w0]
            enter_on[...] = reach
            enter_right.start()
        if index == planes - 2:
            if index > 0:
                partial = product(enter[...], mine[w0:b0]) + mine[b0:n0]
            met_left.wait_recv()
            leave[...] = product(reach, met[:size]) + met[size:]
        else:
            if index > 0:
                partial = product(enter[...], mine[w0:b0]) + mine[b0:n0]
            prepare()
            leave_left.wait_recv()
        if index > 0:
            leave_on[...] = product(leave[...], mine[n0:]) + partial
            leave_left.start()
        if index == planes - 2:
            prepare()
        if index > 0:
            leave_left.wait_send()
        enter_right.wait_send()

    def step_right(index):
        if index < planes - 1:
            met_left.wait_recv()
            turned = product(mine[m0:w0], met[:size])
            turned = jnp.concatenate([turned[:size], turned[size:] + met[size:]], axis=0)
            met_on[...] = product(turned, mine[n0:]) + mine[w0:n0]
            met_left.start()
        enter_right.wait_recv()
        if index < planes - 1:
            reach = product(enter[...], mine[m0:c0]) + mine[c0:w0]
            enter_on[...] = reach
            enter_right.start()
            leave[...] = product(reach, met[:size]) + met[size:]
            enter_right.wait_send()
        else:
            leave[...] = jnp.zeros((sides, size), jnp.float32)
        prepare()
        met_left.wait_send()

    for index in range(planes):
        pl.when(plane == index)(functools.partial(step_left if index < planes - 1 else step_right, index))

    left = left_side(leave[...])
    for s, begin in enumerate(starts):
        y_here = fold(jnp.dot(left, y_maps[s], preferred_element_type=jnp.float32), size) + y_parts[s]
        there = left_side(y_here)
        for i in range(begin, begin + SEGMENT):
            more = jnp.dot(there, maps[1, i], preferred_element_type=jnp.float32)
            out[i] = tails[i, size : size + sides] + fold(more, size)


def on_device(levels, planes, rhs, pivot_inv, lower_gain, upper_gain):
    rows, sides, size = rhs.shape
    depth = len(levels)
    span = 3 * size + 2 * sides
    f32 = jnp.float32
    return pl.pallas_call(
        functools.partial(kernel, levels, planes),
        out_shape=pltpu.VMEM(rhs.shape, f32),
        in_specs=[pl.BlockSpec(memory_space=pltpu.HBM)] * 4,
        out_specs=pl.BlockSpec(memory_space=pltpu.VMEM),
        scratch_shapes=[
            pltpu.VMEM((rows, sides, size), f32),
            pltpu.VMEM((rows, size, size), f32),
            pltpu.VMEM((rows, size, size), f32),
            pltpu.VMEM((rows, size, size), f32),
            pltpu.VMEM((rows, size + sides, size), f32),
            pltpu.VMEM((rows, 2 * size + sides, size), f32),
            pltpu.VMEM((2, rows, 2 * size, 2 * size), jnp.bfloat16),
            pltpu.VMEM((rows // SEGMENT, size + sides, size), f32),
            pltpu.VMEM((rows // SEGMENT, size, size), f32),
            pltpu.VMEM((rows // SEGMENT, size + sides, size), f32),
            pltpu.VMEM((rows // SEGMENT, sides, size), f32),
            pltpu.VMEM((rows // SEGMENT, 2 * size, 2 * size), jnp.bfloat16),
            pltpu.VMEM((depth + 1, 2, span, size), f32),
            pltpu.VMEM((size + sides, size), f32),
            pltpu.VMEM((size, size), f32),
            pltpu.VMEM((size + sides, size), f32),
            pltpu.VMEM((sides, size), f32),
            pltpu.VMEM((sides, size), f32),
            pltpu.VMEM((size + sides, size), f32),
            pltpu.VMEM((sides, size), f32),
            pltpu.VMEM((sides, size), f32),
            pltpu.VMEM((size + sides, size), f32),
            pltpu.SemaphoreType.DMA((4, rows // SEGMENT)),
            pltpu.SemaphoreType.DMA((depth, PARTS)),
            pltpu.SemaphoreType.DMA((depth, PARTS)),
            pltpu.SemaphoreType.DMA((depth, PARTS)),
            pltpu.SemaphoreType.DMA((depth, PARTS)),
            pltpu.SemaphoreType.DMA((3,)),
            pltpu.SemaphoreType.DMA((3,)),
        ],
        compiler_params=pltpu.CompilerParams(
            collective_id=0, has_side_effects=True, vmem_limit_bytes=62 * 2**20
        ),
    )(rhs, pivot_inv, lower_gain, upper_gain)


def solution(mesh):
    levels = []
    planes = min(4, mesh.shape["wide"])
    for axis, count in (("narrow", mesh.shape["narrow"]), ("wide", mesh.shape["wide"] // planes)):
        stride = 1
        while stride < count:
            levels.append((axis, stride))
            stride *= 2
    placed = P(("wide", "narrow"), None, None)
    return jax.shard_map(
        functools.partial(on_device, tuple(levels), planes),
        mesh=mesh,
        in_specs=(placed,) * 4,
        out_specs=placed,
        check_vma=False,
    )
```

```python
import functools

import jax
import jax.numpy as jnp
from jax import lax
from jax.experimental import pallas as pl
from jax.experimental.pallas import tpu as pltpu
from jax.sharding import PartitionSpec as P

MESH = pl.DeviceIdType.MESH
SEGMENT = 3


def halves(value):
    high = value.astype(jnp.bfloat16)
    low = (value - high.astype(jnp.float32)).astype(jnp.bfloat16)
    return high, low


def right_side(value):
    high, low = halves(value)
    row = jnp.concatenate([high, low], axis=1)
    return jnp.concatenate([row, row], axis=0)


def left_side(value):
    high, low = halves(value)
    return jnp.concatenate([high, low], axis=1)


def fold(value, width):
    return value[:, :width] + value[:, width:]


def product(left, right):
    wide = jnp.dot(left_side(left), right_side(right), preferred_element_type=jnp.float32)
    return fold(wide, right.shape[1])


def kernel(
    levels,
    planes,
    rhs_hbm,
    pivot_hbm,
    lower_hbm,
    upper_hbm,
    out,
    rhs,
    pivot,
    lower,
    upper,
    ahead,
    tails,
    maps,
    seg_into,
    seg_leaves,
    seg_cross,
    y_parts,
    y_maps,
    group,
    fp,
    fq,
    fs,
    enter,
    leave,
    met,
    enter_on,
    leave_on,
    met_on,
    load_sem,
    send_sem,
    recv_sem,
    chain_send_sem,
    chain_recv_sem,
):
    rows, sides, size = rhs.shape
    m0, c0, w0, b0, n0, end = 0, size, size + sides, 2 * size + sides, 2 * (size + sides), 3 * size + 2 * sides
    names = ("wide", "narrow")
    place = {name: lax.axis_index(name) for name in names}
    depth = len(levels)

    segments = rows // SEGMENT
    loads = []
    for kind, (source, target) in enumerate(
        ((rhs_hbm, rhs), (pivot_hbm, pivot), (lower_hbm, lower), (upper_hbm, upper))
    ):
        for piece in range(segments):
            span = pl.ds(piece * SEGMENT, SEGMENT)
            load = pltpu.make_async_copy(source.at[span], target.at[span], load_sem.at[kind, piece])
            load.start()
            loads.append(load)

    def partner(level):
        axis, stride = levels[level]
        mine = place[axis]
        side = lax.rem(lax.div(mine, stride), 2)
        other = mine + stride - 2 * stride * side
        return side, tuple(other if name == axis else place[name] for name in names)

    hop = lax.axis_size("wide") // planes
    plane = lax.div(place["wide"], hop)
    before = (place["wide"] - hop, place["narrow"])
    after = (place["wide"] + hop, place["narrow"])

    barrier = pltpu.get_barrier_semaphore()
    for level in range(depth):
        pl.semaphore_signal(barrier, inc=1, device_id=partner(level)[1], device_id_type=MESH)

    @pl.when(plane > 0)
    def _():
        pl.semaphore_signal(barrier, inc=1, device_id=before, device_id_type=MESH)

    @pl.when(plane < planes - 1)
    def _():
        pl.semaphore_signal(barrier, inc=1, device_id=after, device_id_type=MESH)

    for load in loads[: 2 * segments]:
        load.wait()
    for i in range(rows):
        ahead[i, size:] = product(rhs[i], pivot[i])
    for load in loads[2 * segments :]:
        load.wait()

    starts = [segment * SEGMENT for segment in range(segments)]
    fronts, backs = [], []
    for begin in starts:
        fronts.append(jnp.concatenate([-lower[begin], ahead[begin, size:]], axis=0))
        ahead[begin, :size] = fronts[-1][:size]
        backs.append(-upper[begin + SEGMENT - 1])
        tails[begin + SEGMENT - 1, size + sides :] = backs[-1]
    for k in range(1, SEGMENT):
        for s, begin in enumerate(starts):
            i, j = begin + k, begin + SEGMENT - 1 - k
            step = product(fronts[s], lower[i])
            fronts[s] = jnp.concatenate([-step[:size], ahead[i, size:] - step[size:]], axis=0)
            ahead[i] = fronts[s]
            backs[s] = -product(backs[s], upper[j])
            tails[j, size + sides :] = backs[s]
    totals = list(fronts)
    for s, begin in enumerate(starts):
        tails[begin + SEGMENT - 1, : size + sides] = totals[s]
    for k in range(1, SEGMENT):
        for s, begin in enumerate(starts):
            j = begin + SEGMENT - 1 - k
            totals[s] = ahead[j] - product(totals[s], upper[j])
            tails[j, : size + sides] = totals[s]

    def compose(front, first_total, second_front, second_total, get_backs):
        joined = jnp.dot(
            left_side(front),
            jnp.concatenate([right_side(second_front[:size]), right_side(second_total[:size])], axis=1),
            preferred_element_type=jnp.float32,
        )
        onward = add_offset(fold(joined[:, : 2 * size], size), second_front[size:])
        turned = add_offset(fold(joined[:, 2 * size :], size), second_total[size:])
        first_back, second_back = get_backs()
        turned = jnp.concatenate([turned, second_back], axis=0)
        returned = product(turned, first_back)
        return onward, first_total + returned[: size + sides], returned[size + sides :], turned

    def add_offset(value, offset):
        return jnp.concatenate([value[:size], value[size:] + offset], axis=0)

    spans = [(fronts[s], totals[s], backs[s]) for s in range(segments)]
    joins = []
    while len(spans) > 1:
        made = [
            compose(*spans[k][:2], *spans[k + 1][:2], lambda k=k: (spans[k][2], spans[k + 1][2]))
            for k in range(0, len(spans), 2)
        ]
        joins.append([(spans[2 * k][0], made[k][3]) for k in range(len(made))])
        spans = [one[:3] for one in made]
    local_front, local_total, local_back = spans[0]

    inner = (plane > 0).astype(jnp.int32) + (plane < planes - 1).astype(jnp.int32)
    pl.semaphore_wait(barrier, depth + inner)

    def exchange(level):
        side, other = partner(level)
        return [
            pltpu.make_async_remote_copy(
                src_ref=group.at[level, side, span],
                dst_ref=group.at[level, side, span],
                send_sem=send_sem.at[level, k],
                recv_sem=recv_sem.at[level, k],
                device_id=other,
                device_id_type=MESH,
            )
            for k, span in enumerate((pl.ds(m0, n0 - m0), pl.ds(n0, end - n0)))
        ]

    side = partner(0)[0]
    group[0, side, m0:w0] = local_front
    group[0, side, w0:n0] = local_total
    group[0, side, n0:] = local_back
    copies = exchange(0)
    for copy in copies:
        copy.start()

    into, leaves, crosses = [None] * segments, [None] * segments, [None] * segments
    for level, pairs in enumerate(joins):
        for s in range(segments):
            front, turned = pairs[s >> (level + 1)]
            if (s >> level) & 1 == 0:
                if leaves[s] is None:
                    more = turned
                else:
                    more = product(turned, leaves[s])
                leaves[s] = more[size + sides :]
                cross = more[: size + sides]
                crosses[s] = cross if crosses[s] is None else crosses[s] + cross
            else:
                into[s] = front if into[s] is None else add_offset(product(front, into[s][:size]), into[s][size:])
                if crosses[s] is not None:
                    crosses[s] = add_offset(product(front, crosses[s][:size]), crosses[s][size:])
    has_into = [value is not None for value in into]
    has_leaves = [value is not None for value in leaves]
    has_cross = [value is not None for value in crosses]
    for s in range(segments):
        if has_into[s]:
            seg_into[s] = into[s]
        if has_leaves[s]:
            seg_leaves[s] = leaves[s]
        if has_cross[s]:
            seg_cross[s] = crosses[s]

    eye = (
        lax.broadcasted_iota(jnp.int32, (size, size), 0) == lax.broadcasted_iota(jnp.int32, (size, size), 1)
    ).astype(jnp.float32)
    fp[:size] = eye
    fp[size:] = jnp.zeros((sides, size), jnp.float32)
    fq[...] = eye
    fs[...] = jnp.zeros((size + sides, size), jnp.float32)

    def hand(kind, source, target, device):
        return pltpu.make_async_remote_copy(
            src_ref=source,
            dst_ref=target,
            send_sem=chain_send_sem.at[kind],
            recv_sem=chain_recv_sem.at[kind],
            device_id=device,
            device_id_type=MESH,
        )

    enter_right = hand(0, enter_on, enter, after)
    met_left = hand(1, met_on, met, before)
    leave_left = hand(2, leave_on, leave, before)

    def backs_of(copies, first, second):
        def get_backs():
            copies[1].wait_recv()
            return first[n0:], second[n0:]

        return get_backs

    for level in range(depth):
        copies[0].wait_recv()
        side = partner(level)[0]
        first, second = group.at[level, 0], group.at[level, 1]
        front = first[m0:w0]
        onward, total, back, turned = compose(
            front, first[w0:n0], second[m0:w0], second[w0:n0], backs_of(copies, first, second)
        )
        for copy in copies:
            copy.wait_send()
        following = partner(level + 1)[0] if level < depth - 1 else 0
        group[level + 1, following, m0:w0] = onward
        group[level + 1, following, w0:n0] = total
        group[level + 1, following, n0:] = back
        if level < depth - 1:
            copies = exchange(level + 1)
            for copy in copies:
                copy.start()
        else:

            @pl.when(plane == 0)
            def _():
                enter_on[...] = group[depth, 0, c0:w0]
                enter_right.start()

            @pl.when(plane == planes - 1)
            def _():
                met_on[...] = group[depth, 0, w0:n0]
                met_left.start()

        if level == 0:
            for i in range(rows):
                maps[0, i] = right_side(tails[i, :size])
                maps[1, i] = right_side(tails[i, size + sides :])

        @pl.when(side == 0)
        def _():
            more = product(turned, fq[...])
            fs[...] = fs[...] + more[: size + sides]
            fq[...] = more[size + sides :]

        @pl.when(side == 1)
        def _():
            more = product(front, fp[:size])
            fp[size:] = fp[size:] + more[size:]
            fp[:size] = more[:size]
            more = product(front, fs[:size])
            fs[size:] = fs[size:] + more[size:]
            fs[:size] = more[:size]

    def prepare():
        x_in = product(enter[...], fp[:size]) + fp[size:]
        y_part = product(enter[...], fs[:size]) + fs[size:]
        for s, begin in enumerate(starts):
            x_here = x_in
            if has_into[s]:
                x_here = product(x_in, seg_into[s, :size]) + seg_into[s, size:]
            y_here = y_part
            back = fq[...]
            if has_leaves[s]:
                both = product(jnp.concatenate([y_part, back], axis=0), seg_leaves[s])
                y_here, back = both[:sides], both[sides:]
            if has_cross[s]:
                y_here = y_here + product(x_in, seg_cross[s, :size]) + seg_cross[s, size:]
            y_parts[s] = y_here
            y_maps[s] = right_side(back)
            left = left_side(x_here)
            for i in range(begin, begin + SEGMENT):
                more = jnp.dot(left, maps[0, i], preferred_element_type=jnp.float32)
                tails[i, size : size + sides] = tails[i, size : size + sides] + fold(more, size)

    mine = group.at[depth, 0]

    def step_left(index):
        if index == 0:
            enter[...] = jnp.zeros((sides, size), jnp.float32)
            reach = mine[c0:w0]
        else:
            enter_right.wait_recv()
            reach = product(enter[...], mine[m0:c0]) + mine[c0:w0]
            enter_on[...] = reach
            enter_right.start()
        if index == planes - 2:
            if index > 0:
                partial = product(enter[...], mine[w0:b0]) + mine[b0:n0]
            met_left.wait_recv()
            leave[...] = product(reach, met[:size]) + met[size:]
        else:
            if index > 0:
                partial = product(enter[...], mine[w0:b0]) + mine[b0:n0]
            prepare()
            leave_left.wait_recv()
        if index > 0:
            leave_on[...] = product(leave[...], mine[n0:]) + partial
            leave_left.start()
        if index == planes - 2:
            prepare()
        if index > 0:
            leave_left.wait_send()
        enter_right.wait_send()

    def step_right(index):
        if index < planes - 1:
            met_left.wait_recv()
            turned = product(mine[m0:w0], met[:size])
            turned = jnp.concatenate([turned[:size], turned[size:] + met[size:]], axis=0)
            met_on[...] = product(turned, mine[n0:]) + mine[w0:n0]
            met_left.start()
        enter_right.wait_recv()
        if index < planes - 1:
            reach = product(enter[...], mine[m0:c0]) + mine[c0:w0]
            enter_on[...] = reach
            enter_right.start()
            leave[...] = product(reach, met[:size]) + met[size:]
            enter_right.wait_send()
        else:
            leave[...] = jnp.zeros((sides, size), jnp.float32)
        prepare()
        met_left.wait_send()

    for index in range(planes):
        pl.when(plane == index)(functools.partial(step_left if index < planes - 1 else step_right, index))

    left = left_side(leave[...])
    for s, begin in enumerate(starts):
        y_here = fold(jnp.dot(left, y_maps[s], preferred_element_type=jnp.float32), size) + y_parts[s]
        there = left_side(y_here)
        for i in range(begin, begin + SEGMENT):
            more = jnp.dot(there, maps[1, i], preferred_element_type=jnp.float32)
            out[i] = tails[i, size : size + sides] + fold(more, size)


def on_device(levels, planes, rhs, pivot_inv, lower_gain, upper_gain):
    rows, sides, size = rhs.shape
    depth = len(levels)
    span = 3 * size + 2 * sides
    f32 = jnp.float32
    return pl.pallas_call(
        functools.partial(kernel, levels, planes),
        out_shape=pltpu.VMEM(rhs.shape, f32),
        in_specs=[pl.BlockSpec(memory_space=pltpu.HBM)] * 4,
        out_specs=pl.BlockSpec(memory_space=pltpu.VMEM),
        scratch_shapes=[
            pltpu.VMEM((rows, sides, size), f32),
            pltpu.VMEM((rows, size, size), f32),
            pltpu.VMEM((rows, size, size), f32),
            pltpu.VMEM((rows, size, size), f32),
            pltpu.VMEM((rows, size + sides, size), f32),
            pltpu.VMEM((rows, 2 * size + sides, size), f32),
            pltpu.VMEM((2, rows, 2 * size, 2 * size), jnp.bfloat16),
            pltpu.VMEM((rows // SEGMENT, size + sides, size), f32),
            pltpu.VMEM((rows // SEGMENT, size, size), f32),
            pltpu.VMEM((rows // SEGMENT, size + sides, size), f32),
            pltpu.VMEM((rows // SEGMENT, sides, size), f32),
            pltpu.VMEM((rows // SEGMENT, 2 * size, 2 * size), jnp.bfloat16),
            pltpu.VMEM((depth + 1, 2, span, size), f32),
            pltpu.VMEM((size + sides, size), f32),
            pltpu.VMEM((size, size), f32),
            pltpu.VMEM((size + sides, size), f32),
            pltpu.VMEM((sides, size), f32),
            pltpu.VMEM((sides, size), f32),
            pltpu.VMEM((size + sides, size), f32),
            pltpu.VMEM((sides, size), f32),
            pltpu.VMEM((sides, size), f32),
            pltpu.VMEM((size + sides, size), f32),
            pltpu.SemaphoreType.DMA((4, rows // SEGMENT)),
            pltpu.SemaphoreType.DMA((depth, 2)),
            pltpu.SemaphoreType.DMA((depth, 2)),
            pltpu.SemaphoreType.DMA((3,)),
            pltpu.SemaphoreType.DMA((3,)),
        ],
        compiler_params=pltpu.CompilerParams(
            collective_id=0, has_side_effects=True, vmem_limit_bytes=62 * 2**20
        ),
    )(rhs, pivot_inv, lower_gain, upper_gain)


def solution(mesh):
    levels = []
    planes = min(4, mesh.shape["wide"])
    for axis, count in (("narrow", mesh.shape["narrow"]), ("wide", mesh.shape["wide"] // planes)):
        stride = 1
        while stride < count:
            levels.append((axis, stride))
            stride *= 2
    placed = P(("wide", "narrow"), None, None)
    return jax.shard_map(
        functools.partial(on_device, tuple(levels), planes),
        mesh=mesh,
        in_specs=(placed,) * 4,
        out_specs=placed,
        check_vma=False,
    )
```

```python
import functools

import jax
import jax.numpy as jnp
from jax import lax
from jax.experimental import pallas as pl
from jax.experimental.pallas import tpu as pltpu
from jax.sharding import PartitionSpec as P

MESH = pl.DeviceIdType.MESH
SEGMENT = 3
PARTS = 4


def halves(value):
    high = value.astype(jnp.bfloat16)
    low = (value - high.astype(jnp.float32)).astype(jnp.bfloat16)
    return high, low


def right_side(value):
    high, low = halves(value)
    row = jnp.concatenate([high, low], axis=1)
    return jnp.concatenate([row, row], axis=0)


def left_side(value):
    high, low = halves(value)
    return jnp.concatenate([high, low], axis=1)


def fold(value, width):
    return value[:, :width] + value[:, width:]


def product(left, right):
    wide = jnp.dot(left_side(left), right_side(right), preferred_element_type=jnp.float32)
    return fold(wide, right.shape[1])


def kernel(
    levels,
    planes,
    rhs_hbm,
    pivot_hbm,
    lower_hbm,
    upper_hbm,
    out,
    rhs,
    pivot,
    lower,
    upper,
    ahead,
    tails,
    maps,
    seg_into,
    seg_leaves,
    seg_cross,
    y_parts,
    y_maps,
    group,
    fp,
    fq,
    fs,
    enter,
    leave,
    met,
    enter_on,
    leave_on,
    met_on,
    load_sem,
    send_sem,
    recv_sem,
    pass_send_sem,
    pass_recv_sem,
    chain_send_sem,
    chain_recv_sem,
):
    rows, sides, size = rhs.shape
    m0, c0, w0, b0, n0, end = 0, size, size + sides, 2 * size + sides, 2 * (size + sides), 3 * size + 2 * sides
    names = ("wide", "narrow")
    place = {name: lax.axis_index(name) for name in names}
    depth = len(levels)

    segments = rows // SEGMENT
    loads = []
    for kind, (source, target) in enumerate(
        ((rhs_hbm, rhs), (pivot_hbm, pivot), (lower_hbm, lower), (upper_hbm, upper))
    ):
        for piece in range(segments):
            span = pl.ds(piece * SEGMENT, SEGMENT)
            load = pltpu.make_async_copy(source.at[span], target.at[span], load_sem.at[kind, piece])
            load.start()
            loads.append(load)

    def partner(level):
        axis, stride = levels[level]
        mine = place[axis]
        side = lax.rem(lax.div(mine, stride), 2)
        other = mine + stride - 2 * stride * side
        return side, tuple(other if name == axis else place[name] for name in names)

    hop = lax.axis_size("wide") // planes
    plane = lax.div(place["wide"], hop)
    before = (place["wide"] - hop, place["narrow"])
    after = (place["wide"] + hop, place["narrow"])
    sibling = (place["wide"], 1 - place["narrow"])

    barrier = pltpu.get_barrier_semaphore()
    for level in range(depth):
        pl.semaphore_signal(barrier, inc=1, device_id=partner(level)[1], device_id_type=MESH)

    @pl.when(plane > 0)
    def _():
        pl.semaphore_signal(barrier, inc=1, device_id=before, device_id_type=MESH)

    @pl.when(plane < planes - 1)
    def _():
        pl.semaphore_signal(barrier, inc=1, device_id=after, device_id_type=MESH)

    for load in loads[: 2 * segments]:
        load.wait()
    for i in range(rows):
        ahead[i, size:] = product(rhs[i], pivot[i])
    for load in loads[2 * segments :]:
        load.wait()

    starts = [segment * SEGMENT for segment in range(segments)]
    fronts, backs = [], []
    for begin in starts:
        fronts.append(jnp.concatenate([-lower[begin], ahead[begin, size:]], axis=0))
        ahead[begin, :size] = fronts[-1][:size]
        backs.append(-upper[begin + SEGMENT - 1])
        tails[begin + SEGMENT - 1, size + sides :] = backs[-1]
    for k in range(1, SEGMENT):
        for s, begin in enumerate(starts):
            i, j = begin + k, begin + SEGMENT - 1 - k
            step = product(fronts[s], lower[i])
            fronts[s] = jnp.concatenate([-step[:size], ahead[i, size:] - step[size:]], axis=0)
            ahead[i] = fronts[s]
            backs[s] = -product(backs[s], upper[j])
            tails[j, size + sides :] = backs[s]
    totals = list(fronts)
    for s, begin in enumerate(starts):
        tails[begin + SEGMENT - 1, : size + sides] = totals[s]
    for k in range(1, SEGMENT):
        for s, begin in enumerate(starts):
            j = begin + SEGMENT - 1 - k
            totals[s] = ahead[j] - product(totals[s], upper[j])
            tails[j, : size + sides] = totals[s]

    def compose(front, first_total, second_front, second_total, get_backs):
        joined = jnp.dot(
            left_side(front),
            jnp.concatenate([right_side(second_front[:size]), right_side(second_total[:size])], axis=1),
            preferred_element_type=jnp.float32,
        )
        onward = add_offset(fold(joined[:, : 2 * size], size), second_front[size:])
        turned = add_offset(fold(joined[:, 2 * size :], size), second_total[size:])
        first_back, second_back = get_backs()
        turned = jnp.concatenate([turned, second_back], axis=0)
        returned = product(turned, first_back)
        return onward, first_total + returned[: size + sides], returned[size + sides :], turned

    def add_offset(value, offset):
        return jnp.concatenate([value[:size], value[size:] + offset], axis=0)

    spans = [(fronts[s], totals[s], backs[s]) for s in range(segments)]
    joins = []
    while len(spans) > 1:
        made = [
            compose(*spans[k][:2], *spans[k + 1][:2], lambda k=k: (spans[k][2], spans[k + 1][2]))
            for k in range(0, len(spans), 2)
        ]
        joins.append([(spans[2 * k][0], made[k][3]) for k in range(len(made))])
        spans = [one[:3] for one in made]
    local_front, local_total, local_back = spans[0]

    inner = (plane > 0).astype(jnp.int32) + (plane < planes - 1).astype(jnp.int32)
    pl.semaphore_wait(barrier, depth + inner)

    part = end // (2 * PARTS)

    def wave(k):
        return pl.ds(pl.multiple_of((2 * k + place["narrow"]) * part, part), part)

    def exchange(level):
        side, other = partner(level)
        if levels[level][0] == "narrow":
            spans = [pl.ds(0, end)]
        else:
            spans = [wave(k) for k in range(PARTS)]
        return [
            pltpu.make_async_remote_copy(
                src_ref=group.at[level, side, span],
                dst_ref=group.at[level, side, span],
                send_sem=send_sem.at[level, k],
                recv_sem=recv_sem.at[level, k],
                device_id=other,
                device_id_type=MESH,
            )
            for k, span in enumerate(spans)
        ]

    def finish(level, copies):
        if levels[level][0] == "narrow":
            copies[0].wait()
            return None
        side = partner(level)[0]
        relays = []
        for k, copy in enumerate(copies):
            copy.wait_recv()
            relay = pltpu.make_async_remote_copy(
                src_ref=group.at[level, 1 - side, wave(k)],
                dst_ref=group.at[level, 1 - side, wave(k)],
                send_sem=pass_send_sem.at[level, k],
                recv_sem=pass_recv_sem.at[level, k],
                device_id=sibling,
                device_id_type=MESH,
            )
            relay.start()
            relays.append(relay)
        for relay in relays[:-1]:
            relay.wait_recv()
        return relays

    side = partner(0)[0]
    group[0, side, m0:w0] = local_front
    group[0, side, w0:n0] = local_total
    group[0, side, n0:] = local_back
    copies = exchange(0)
    for copy in copies:
        copy.start()

    into, leaves, crosses = [None] * segments, [None] * segments, [None] * segments
    for level, pairs in enumerate(joins):
        for s in range(segments):
            front, turned = pairs[s >> (level + 1)]
            if (s >> level) & 1 == 0:
                if leaves[s] is None:
                    more = turned
                else:
                    more = product(turned, leaves[s])
                leaves[s] = more[size + sides :]
                cross = more[: size + sides]
                crosses[s] = cross if crosses[s] is None else crosses[s] + cross
            else:
                into[s] = front if into[s] is None else add_offset(product(front, into[s][:size]), into[s][size:])
                if crosses[s] is not None:
                    crosses[s] = add_offset(product(front, crosses[s][:size]), crosses[s][size:])
    has_into = [value is not None for value in into]
    has_leaves = [value is not None for value in leaves]
    has_cross = [value is not None for value in crosses]
    for s in range(segments):
        if has_into[s]:
            seg_into[s] = into[s]
        if has_leaves[s]:
            seg_leaves[s] = leaves[s]
        if has_cross[s]:
            seg_cross[s] = crosses[s]

    eye = (
        lax.broadcasted_iota(jnp.int32, (size, size), 0) == lax.broadcasted_iota(jnp.int32, (size, size), 1)
    ).astype(jnp.float32)
    fp[:size] = eye
    fp[size:] = jnp.zeros((sides, size), jnp.float32)
    fq[...] = eye
    fs[...] = jnp.zeros((size + sides, size), jnp.float32)

    def hand(kind, source, target, device):
        return pltpu.make_async_remote_copy(
            src_ref=source,
            dst_ref=target,
            send_sem=chain_send_sem.at[kind],
            recv_sem=chain_recv_sem.at[kind],
            device_id=device,
            device_id_type=MESH,
        )

    enter_right = hand(0, enter_on, enter, after)
    met_left = hand(1, met_on, met, before)
    leave_left = hand(2, leave_on, leave, before)

    def backs_of(relays, first, second):
        def get_backs():
            if relays is not None:
                relays[-1].wait_recv()
            return first[n0:], second[n0:]

        return get_backs

    for level in range(depth):
        relays = finish(level, copies)
        side = partner(level)[0]
        first, second = group.at[level, 0], group.at[level, 1]
        front = first[m0:w0]
        onward, total, back, turned = compose(
            front, first[w0:n0], second[m0:w0], second[w0:n0], backs_of(relays, first, second)
        )
        if relays is not None:
            for copy in copies + relays:
                copy.wait_send()
        following = partner(level + 1)[0] if level < depth - 1 else 0
        group[level + 1, following, m0:w0] = onward
        group[level + 1, following, w0:n0] = total
        group[level + 1, following, n0:] = back
        if level < depth - 1:
            copies = exchange(level + 1)
            for copy in copies:
                copy.start()
        else:

            @pl.when(plane == 0)
            def _():
                enter_on[...] = group[depth, 0, c0:w0]
                enter_right.start()

            @pl.when(plane == planes - 1)
            def _():
                met_on[...] = group[depth, 0, w0:n0]
                met_left.start()

        if level == 0:
            for i in range(rows):
                maps[0, i] = right_side(tails[i, :size])
                maps[1, i] = right_side(tails[i, size + sides :])

        @pl.when(side == 0)
        def _():
            more = product(turned, fq[...])
            fs[...] = fs[...] + more[: size + sides]
            fq[...] = more[size + sides :]

        @pl.when(side == 1)
        def _():
            more = product(front, fp[:size])
            fp[size:] = fp[size:] + more[size:]
            fp[:size] = more[:size]
            more = product(front, fs[:size])
            fs[size:] = fs[size:] + more[size:]
            fs[:size] = more[:size]

    def prepare():
        x_in = product(enter[...], fp[:size]) + fp[size:]
        y_part = product(enter[...], fs[:size]) + fs[size:]
        for s, begin in enumerate(starts):
            x_here = x_in
            if has_into[s]:
                x_here = product(x_in, seg_into[s, :size]) + seg_into[s, size:]
            y_here = y_part
            back = fq[...]
            if has_leaves[s]:
                both = product(jnp.concatenate([y_part, back], axis=0), seg_leaves[s])
                y_here, back = both[:sides], both[sides:]
            if has_cross[s]:
                y_here = y_here + product(x_in, seg_cross[s, :size]) + seg_cross[s, size:]
            y_parts[s] = y_here
            y_maps[s] = right_side(back)
            left = left_side(x_here)
            for i in range(begin, begin + SEGMENT):
                more = jnp.dot(left, maps[0, i], preferred_element_type=jnp.float32)
                tails[i, size : size + sides] = tails[i, size : size + sides] + fold(more, size)

    mine = group.at[depth, 0]

    def step_left(index):
        if index == 0:
            enter[...] = jnp.zeros((sides, size), jnp.float32)
            reach = mine[c0:w0]
        else:
            enter_right.wait_recv()
            reach = product(enter[...], mine[m0:c0]) + mine[c0:w0]
            enter_on[...] = reach
            enter_right.start()
        if index == planes - 2:
            if index > 0:
                partial = product(enter[...], mine[w0:b0]) + mine[b0:n0]
            met_left.wait_recv()
            leave[...] = product(reach, met[:size]) + met[size:]
        else:
            if index > 0:
                partial = product(enter[...], mine[w0:b0]) + mine[b0:n0]
            prepare()
            leave_left.wait_recv()
        if index > 0:
            leave_on[...] = product(leave[...], mine[n0:]) + partial
            leave_left.start()
        if index == planes - 2:
            prepare()
        if index > 0:
            leave_left.wait_send()
        enter_right.wait_send()

    def step_right(index):
        if index < planes - 1:
            met_left.wait_recv()
            turned = product(mine[m0:w0], met[:size])
            turned = jnp.concatenate([turned[:size], turned[size:] + met[size:]], axis=0)
            met_on[...] = product(turned, mine[n0:]) + mine[w0:n0]
            met_left.start()
        enter_right.wait_recv()
        if index < planes - 1:
            reach = product(enter[...], mine[m0:c0]) + mine[c0:w0]
            enter_on[...] = reach
            enter_right.start()
            leave[...] = product(reach, met[:size]) + met[size:]
            enter_right.wait_send()
        else:
            leave[...] = jnp.zeros((sides, size), jnp.float32)
        prepare()
        met_left.wait_send()

    for index in range(planes):
        pl.when(plane == index)(functools.partial(step_left if index < planes - 1 else step_right, index))

    left = left_side(leave[...])
    for s, begin in enumerate(starts):
        y_here = fold(jnp.dot(left, y_maps[s], preferred_element_type=jnp.float32), size) + y_parts[s]
        there = left_side(y_here)
        for i in range(begin, begin + SEGMENT):
            more = jnp.dot(there, maps[1, i], preferred_element_type=jnp.float32)
            out[i] = tails[i, size : size + sides] + fold(more, size)


def on_device(levels, planes, rhs, pivot_inv, lower_gain, upper_gain):
    rows, sides, size = rhs.shape
    depth = len(levels)
    span = 3 * size + 2 * sides
    f32 = jnp.float32
    return pl.pallas_call(
        functools.partial(kernel, levels, planes),
        out_shape=pltpu.VMEM(rhs.shape, f32),
        in_specs=[pl.BlockSpec(memory_space=pltpu.HBM)] * 4,
        out_specs=pl.BlockSpec(memory_space=pltpu.VMEM),
        scratch_shapes=[
            pltpu.VMEM((rows, sides, size), f32),
            pltpu.VMEM((rows, size, size), f32),
            pltpu.VMEM((rows, size, size), f32),
            pltpu.VMEM((rows, size, size), f32),
            pltpu.VMEM((rows, size + sides, size), f32),
            pltpu.VMEM((rows, 2 * size + sides, size), f32),
            pltpu.VMEM((2, rows, 2 * size, 2 * size), jnp.bfloat16),
            pltpu.VMEM((rows // SEGMENT, size + sides, size), f32),
            pltpu.VMEM((rows // SEGMENT, size, size), f32),
            pltpu.VMEM((rows // SEGMENT, size + sides, size), f32),
            pltpu.VMEM((rows // SEGMENT, sides, size), f32),
            pltpu.VMEM((rows // SEGMENT, 2 * size, 2 * size), jnp.bfloat16),
            pltpu.VMEM((depth + 1, 2, span, size), f32),
            pltpu.VMEM((size + sides, size), f32),
            pltpu.VMEM((size, size), f32),
            pltpu.VMEM((size + sides, size), f32),
            pltpu.VMEM((sides, size), f32),
            pltpu.VMEM((sides, size), f32),
            pltpu.VMEM((size + sides, size), f32),
            pltpu.VMEM((sides, size), f32),
            pltpu.VMEM((sides, size), f32),
            pltpu.VMEM((size + sides, size), f32),
            pltpu.SemaphoreType.DMA((4, rows // SEGMENT)),
            pltpu.SemaphoreType.DMA((depth, PARTS)),
            pltpu.SemaphoreType.DMA((depth, PARTS)),
            pltpu.SemaphoreType.DMA((depth, PARTS)),
            pltpu.SemaphoreType.DMA((depth, PARTS)),
            pltpu.SemaphoreType.DMA((3,)),
            pltpu.SemaphoreType.DMA((3,)),
        ],
        compiler_params=pltpu.CompilerParams(
            collective_id=0, has_side_effects=True, vmem_limit_bytes=62 * 2**20
        ),
    )(rhs, pivot_inv, lower_gain, upper_gain)


def solution(mesh):
    levels = []
    planes = min(4, mesh.shape["wide"])
    for axis, count in (("narrow", mesh.shape["narrow"]), ("wide", mesh.shape["wide"] // planes)):
        stride = 1
        while stride < count:
            levels.append((axis, stride))
            stride *= 2
    placed = P(("wide", "narrow"), None, None)
    return jax.shard_map(
        functools.partial(on_device, tuple(levels), planes),
        mesh=mesh,
        in_specs=(placed,) * 4,
        out_specs=placed,
        check_vma=False,
    )
```

```python
import functools

import jax
import jax.numpy as jnp
from jax import lax
from jax.experimental import pallas as pl
from jax.experimental.pallas import tpu as pltpu
from jax.sharding import PartitionSpec as P

MESH = pl.DeviceIdType.MESH
SEGMENT = 3
PARTS = 2


def halves(value):
    high = value.astype(jnp.bfloat16)
    low = (value - high.astype(jnp.float32)).astype(jnp.bfloat16)
    return high, low


def right_side(value):
    high, low = halves(value)
    row = jnp.concatenate([high, low], axis=1)
    return jnp.concatenate([row, row], axis=0)


def left_side(value):
    high, low = halves(value)
    return jnp.concatenate([high, low], axis=1)


def fold(value, width):
    return value[:, :width] + value[:, width:]


def product(left, right):
    wide = jnp.dot(left_side(left), right_side(right), preferred_element_type=jnp.float32)
    return fold(wide, right.shape[1])


def kernel(
    levels,
    planes,
    rhs_hbm,
    pivot_hbm,
    lower_hbm,
    upper_hbm,
    out,
    rhs,
    pivot,
    lower,
    upper,
    ahead,
    tails,
    maps,
    seg_into,
    seg_leaves,
    seg_cross,
    y_parts,
    y_maps,
    group,
    fp,
    fq,
    fs,
    enter,
    leave,
    met,
    enter_on,
    leave_on,
    met_on,
    load_sem,
    send_sem,
    recv_sem,
    pass_send_sem,
    pass_recv_sem,
    chain_send_sem,
    chain_recv_sem,
):
    rows, sides, size = rhs.shape
    m0, c0, w0, b0, n0, end = 0, size, size + sides, 2 * size + sides, 2 * (size + sides), 3 * size + 2 * sides
    names = ("wide", "narrow")
    place = {name: lax.axis_index(name) for name in names}
    depth = len(levels)

    segments = rows // SEGMENT
    loads = []
    for kind, (source, target) in enumerate(
        ((rhs_hbm, rhs), (pivot_hbm, pivot), (lower_hbm, lower), (upper_hbm, upper))
    ):
        for piece in range(segments):
            span = pl.ds(piece * SEGMENT, SEGMENT)
            load = pltpu.make_async_copy(source.at[span], target.at[span], load_sem.at[kind, piece])
            load.start()
            loads.append(load)

    def partner(level):
        axis, stride = levels[level]
        mine = place[axis]
        side = lax.rem(lax.div(mine, stride), 2)
        other = mine + stride - 2 * stride * side
        return side, tuple(other if name == axis else place[name] for name in names)

    hop = lax.axis_size("wide") // planes
    plane = lax.div(place["wide"], hop)
    before = (place["wide"] - hop, place["narrow"])
    after = (place["wide"] + hop, place["narrow"])
    sibling = (place["wide"], 1 - place["narrow"])

    barrier = pltpu.get_barrier_semaphore()
    for level in range(depth):
        pl.semaphore_signal(barrier, inc=1, device_id=partner(level)[1], device_id_type=MESH)

    @pl.when(plane > 0)
    def _():
        pl.semaphore_signal(barrier, inc=1, device_id=before, device_id_type=MESH)

    @pl.when(plane < planes - 1)
    def _():
        pl.semaphore_signal(barrier, inc=1, device_id=after, device_id_type=MESH)

    for load in loads[: 2 * segments]:
        load.wait()
    for i in range(rows):
        ahead[i, size:] = product(rhs[i], pivot[i])
    for load in loads[2 * segments :]:
        load.wait()

    starts = [segment * SEGMENT for segment in range(segments)]
    fronts, backs = [], []
    for begin in starts:
        fronts.append(jnp.concatenate([-lower[begin], ahead[begin, size:]], axis=0))
        ahead[begin, :size] = fronts[-1][:size]
        backs.append(-upper[begin + SEGMENT - 1])
        tails[begin + SEGMENT - 1, size + sides :] = backs[-1]
    for k in range(1, SEGMENT):
        for s, begin in enumerate(starts):
            i, j = begin + k, begin + SEGMENT - 1 - k
            step = product(fronts[s], lower[i])
            fronts[s] = jnp.concatenate([-step[:size], ahead[i, size:] - step[size:]], axis=0)
            ahead[i] = fronts[s]
            backs[s] = -product(backs[s], upper[j])
            tails[j, size + sides :] = backs[s]
    totals = list(fronts)
    for s, begin in enumerate(starts):
        tails[begin + SEGMENT - 1, : size + sides] = totals[s]
    for k in range(1, SEGMENT):
        for s, begin in enumerate(starts):
            j = begin + SEGMENT - 1 - k
            totals[s] = ahead[j] - product(totals[s], upper[j])
            tails[j, : size + sides] = totals[s]

    def compose(front, first_total, first_back, second_front, second_total, second_back):
        joined = jnp.dot(
            left_side(front),
            jnp.concatenate([right_side(second_front[:size]), right_side(second_total[:size])], axis=1),
            preferred_element_type=jnp.float32,
        )
        onward = add_offset(fold(joined[:, : 2 * size], size), second_front[size:])
        turned = add_offset(fold(joined[:, 2 * size :], size), second_total[size:])
        turned = jnp.concatenate([turned, second_back], axis=0)
        returned = product(turned, first_back)
        return onward, first_total + returned[: size + sides], returned[size + sides :], turned

    def add_offset(value, offset):
        return jnp.concatenate([value[:size], value[size:] + offset], axis=0)

    spans = [(fronts[s], totals[s], backs[s]) for s in range(segments)]
    joins = []
    while len(spans) > 1:
        made = [compose(*spans[k], *spans[k + 1]) for k in range(0, len(spans), 2)]
        joins.append([(spans[2 * k][0], made[k][3]) for k in range(len(made))])
        spans = [one[:3] for one in made]
    local_front, local_total, local_back = spans[0]

    inner = (plane > 0).astype(jnp.int32) + (plane < planes - 1).astype(jnp.int32)
    pl.semaphore_wait(barrier, depth + inner)

    part = end // (2 * PARTS)

    def exchange(level):
        side, other = partner(level)
        if levels[level][0] == "narrow":
            spans = [pl.ds(0, end)]
        else:
            begin = place["narrow"] * (end // 2)
            spans = [pl.ds(pl.multiple_of(begin + k * part, part), part) for k in range(PARTS)]
        return [
            pltpu.make_async_remote_copy(
                src_ref=group.at[level, side, span],
                dst_ref=group.at[level, side, span],
                send_sem=send_sem.at[level, k],
                recv_sem=recv_sem.at[level, k],
                device_id=other,
                device_id_type=MESH,
            )
            for k, span in enumerate(spans)
        ]

    def finish(level, copies):
        if levels[level][0] == "narrow":
            copies[0].wait()
            return
        side = partner(level)[0]
        begin = place["narrow"] * (end // 2)
        relays = []
        for k, copy in enumerate(copies):
            copy.wait_recv()
            span = pl.ds(pl.multiple_of(begin + k * part, part), part)
            relay = pltpu.make_async_remote_copy(
                src_ref=group.at[level, 1 - side, span],
                dst_ref=group.at[level, 1 - side, span],
                send_sem=pass_send_sem.at[level, k],
                recv_sem=pass_recv_sem.at[level, k],
                device_id=sibling,
                device_id_type=MESH,
            )
            relay.start()
            relays.append(relay)
        for copy in copies:
            copy.wait_send()
        for relay in relays:
            relay.wait()

    side = partner(0)[0]
    group[0, side, m0:w0] = local_front
    group[0, side, w0:n0] = local_total
    group[0, side, n0:] = local_back
    copies = exchange(0)
    for copy in copies:
        copy.start()

    into, leaves, crosses = [None] * segments, [None] * segments, [None] * segments
    for level, pairs in enumerate(joins):
        for s in range(segments):
            front, turned = pairs[s >> (level + 1)]
            if (s >> level) & 1 == 0:
                if leaves[s] is None:
                    more = turned
                else:
                    more = product(turned, leaves[s])
                leaves[s] = more[size + sides :]
                cross = more[: size + sides]
                crosses[s] = cross if crosses[s] is None else crosses[s] + cross
            else:
                into[s] = front if into[s] is None else add_offset(product(front, into[s][:size]), into[s][size:])
                if crosses[s] is not None:
                    crosses[s] = add_offset(product(front, crosses[s][:size]), crosses[s][size:])
    has_into = [value is not None for value in into]
    has_leaves = [value is not None for value in leaves]
    has_cross = [value is not None for value in crosses]
    for s in range(segments):
        if has_into[s]:
            seg_into[s] = into[s]
        if has_leaves[s]:
            seg_leaves[s] = leaves[s]
        if has_cross[s]:
            seg_cross[s] = crosses[s]

    eye = (
        lax.broadcasted_iota(jnp.int32, (size, size), 0) == lax.broadcasted_iota(jnp.int32, (size, size), 1)
    ).astype(jnp.float32)
    fp[:size] = eye
    fp[size:] = jnp.zeros((sides, size), jnp.float32)
    fq[...] = eye
    fs[...] = jnp.zeros((size + sides, size), jnp.float32)

    def hand(kind, source, target, device):
        return pltpu.make_async_remote_copy(
            src_ref=source,
            dst_ref=target,
            send_sem=chain_send_sem.at[kind],
            recv_sem=chain_recv_sem.at[kind],
            device_id=device,
            device_id_type=MESH,
        )

    enter_right = hand(0, enter_on, enter, after)
    share = pl.ds(pl.multiple_of(place["narrow"] * ((size + sides) // 2), 8), (size + sides) // 2)
    met_left = hand(1, met_on.at[share], met.at[share], before)
    met_across = hand(3, met.at[share], met.at[share], sibling)
    leave_left = hand(2, leave_on, leave, before)

    for level in range(depth):
        finish(level, copies)
        side = partner(level)[0]
        first, second = group.at[level, 0], group.at[level, 1]
        front = first[m0:w0]
        onward, total, back, turned = compose(
            front, first[w0:n0], first[n0:], second[m0:w0], second[w0:n0], second[n0:]
        )
        following = partner(level + 1)[0] if level < depth - 1 else 0
        group[level + 1, following, m0:w0] = onward
        group[level + 1, following, w0:n0] = total
        group[level + 1, following, n0:] = back
        if level < depth - 1:
            copies = exchange(level + 1)
            for copy in copies:
                copy.start()
        else:

            @pl.when(plane == 0)
            def _():
                enter_on[...] = group[depth, 0, c0:w0]
                enter_right.start()

            @pl.when(plane == planes - 1)
            def _():
                met_on[...] = group[depth, 0, w0:n0]
                met_left.start()

        if level == 0:
            for i in range(rows):
                maps[0, i] = right_side(tails[i, :size])
                maps[1, i] = right_side(tails[i, size + sides :])

        @pl.when(side == 0)
        def _():
            more = product(turned, fq[...])
            fs[...] = fs[...] + more[: size + sides]
            fq[...] = more[size + sides :]

        @pl.when(side == 1)
        def _():
            more = product(front, fp[:size])
            fp[size:] = fp[size:] + more[size:]
            fp[:size] = more[:size]
            more = product(front, fs[:size])
            fs[size:] = fs[size:] + more[size:]
            fs[:size] = more[:size]

    def prepare():
        x_in = product(enter[...], fp[:size]) + fp[size:]
        y_part = product(enter[...], fs[:size]) + fs[size:]
        for s, begin in enumerate(starts):
            x_here = x_in
            if has_into[s]:
                x_here = product(x_in, seg_into[s, :size]) + seg_into[s, size:]
            y_here = y_part
            back = fq[...]
            if has_leaves[s]:
                both = product(jnp.concatenate([y_part, back], axis=0), seg_leaves[s])
                y_here, back = both[:sides], both[sides:]
            if has_cross[s]:
                y_here = y_here + product(x_in, seg_cross[s, :size]) + seg_cross[s, size:]
            y_parts[s] = y_here
            y_maps[s] = right_side(back)
            left = left_side(x_here)
            for i in range(begin, begin + SEGMENT):
                more = jnp.dot(left, maps[0, i], preferred_element_type=jnp.float32)
                tails[i, size : size + sides] = tails[i, size : size + sides] + fold(more, size)

    mine = group.at[depth, 0]

    def step_left(index):
        if index == 0:
            enter[...] = jnp.zeros((sides, size), jnp.float32)
            reach = mine[c0:w0]
        else:
            enter_right.wait_recv()
            reach = product(enter[...], mine[m0:c0]) + mine[c0:w0]
            enter_on[...] = reach
            enter_right.start()
        if index == planes - 2:
            if index > 0:
                partial = product(enter[...], mine[w0:b0]) + mine[b0:n0]
            met_left.wait_recv()
            met_across.start()
            met_across.wait()
            leave[...] = product(reach, met[:size]) + met[size:]
        else:
            if index > 0:
                partial = product(enter[...], mine[w0:b0]) + mine[b0:n0]
            prepare()
            leave_left.wait_recv()
        if index > 0:
            leave_on[...] = product(leave[...], mine[n0:]) + partial
            leave_left.start()
        if index == planes - 2:
            prepare()
        if index > 0:
            leave_left.wait_send()
        enter_right.wait_send()

    def step_right(index):
        enter_right.wait_recv()
        leave[...] = jnp.zeros((sides, size), jnp.float32)
        prepare()
        met_left.wait_send()

    for index in range(planes):
        pl.when(plane == index)(functools.partial(step_left if index < planes - 1 else step_right, index))

    left = left_side(leave[...])
    for s, begin in enumerate(starts):
        y_here = fold(jnp.dot(left, y_maps[s], preferred_element_type=jnp.float32), size) + y_parts[s]
        there = left_side(y_here)
        for i in range(begin, begin + SEGMENT):
            more = jnp.dot(there, maps[1, i], preferred_element_type=jnp.float32)
            out[i] = tails[i, size : size + sides] + fold(more, size)


def on_device(levels, planes, rhs, pivot_inv, lower_gain, upper_gain):
    rows, sides, size = rhs.shape
    depth = len(levels)
    span = 3 * size + 2 * sides
    f32 = jnp.float32
    return pl.pallas_call(
        functools.partial(kernel, levels, planes),
        out_shape=pltpu.VMEM(rhs.shape, f32),
        in_specs=[pl.BlockSpec(memory_space=pltpu.HBM)] * 4,
        out_specs=pl.BlockSpec(memory_space=pltpu.VMEM),
        scratch_shapes=[
            pltpu.VMEM((rows, sides, size), f32),
            pltpu.VMEM((rows, size, size), f32),
            pltpu.VMEM((rows, size, size), f32),
            pltpu.VMEM((rows, size, size), f32),
            pltpu.VMEM((rows, size + sides, size), f32),
            pltpu.VMEM((rows, 2 * size + sides, size), f32),
            pltpu.VMEM((2, rows, 2 * size, 2 * size), jnp.bfloat16),
            pltpu.VMEM((rows // SEGMENT, size + sides, size), f32),
            pltpu.VMEM((rows // SEGMENT, size, size), f32),
            pltpu.VMEM((rows // SEGMENT, size + sides, size), f32),
            pltpu.VMEM((rows // SEGMENT, sides, size), f32),
            pltpu.VMEM((rows // SEGMENT, 2 * size, 2 * size), jnp.bfloat16),
            pltpu.VMEM((depth + 1, 2, span, size), f32),
            pltpu.VMEM((size + sides, size), f32),
            pltpu.VMEM((size, size), f32),
            pltpu.VMEM((size + sides, size), f32),
            pltpu.VMEM((sides, size), f32),
            pltpu.VMEM((sides, size), f32),
            pltpu.VMEM((size + sides, size), f32),
            pltpu.VMEM((sides, size), f32),
            pltpu.VMEM((sides, size), f32),
            pltpu.VMEM((size + sides, size), f32),
            pltpu.SemaphoreType.DMA((4, rows // SEGMENT)),
            pltpu.SemaphoreType.DMA((depth, PARTS)),
            pltpu.SemaphoreType.DMA((depth, PARTS)),
            pltpu.SemaphoreType.DMA((depth, PARTS)),
            pltpu.SemaphoreType.DMA((depth, PARTS)),
            pltpu.SemaphoreType.DMA((4,)),
            pltpu.SemaphoreType.DMA((4,)),
        ],
        compiler_params=pltpu.CompilerParams(
            collective_id=0, has_side_effects=True, vmem_limit_bytes=62 * 2**20
        ),
    )(rhs, pivot_inv, lower_gain, upper_gain)


def solution(mesh):
    levels = []
    planes = min(4, mesh.shape["wide"])
    for axis, count in (("narrow", mesh.shape["narrow"]), ("wide", mesh.shape["wide"] // planes)):
        stride = 1
        while stride < count:
            levels.append((axis, stride))
            stride *= 2
    placed = P(("wide", "narrow"), None, None)
    return jax.shard_map(
        functools.partial(on_device, tuple(levels), planes),
        mesh=mesh,
        in_specs=(placed,) * 4,
        out_specs=placed,
        check_vma=False,
    )
```
